512 devices in a mesh: expert: 128 (over z, y, core), tensor: 4 (over x).
Axes of the slice: x: 4, y: 8, z: 8, core: 2. Of those that a mesh axis runs over, the one named last changes fastest.
Arguments:
- tokens: bfloat16 [16384, 2880], P('expert', 'tensor'), may hold values from -6 to 6
- routes: int32 [16384, 4], P('expert'), may hold values from 0 to 127, all different within a row; in each aligned block of 128 rows (0 to 127, 128 to 255, ...) at most 5 rows name the same one
- route_gate_weight: int32 [16384, 4], P('expert'), may hold values from 1 to 65535
- up_frozen_matrix: bfloat16 [128, 2880, 1440], P('expert', None, 'tensor'), may hold values from -0.109375 to 0.109375
- down_frozen_matrix: bfloat16 [128, 1440, 2880], P('expert', 'tensor'), may hold values from -0.15625 to 0.15625
- up_adapter_input: bfloat16 [128, 2880, 64], P('expert', None, 'tensor'), may hold values from -0.109375 to 0.109375
- up_adapter_output: bfloat16 [128, 64, 1440], P('expert', None, 'tensor'), may hold values from -0.75 to 0.75
- down_adapter_input: bfloat16 [128, 1440, 64], P('expert', 'tensor'), may hold values from -0.15625 to 0.15625
- down_adapter_output: bfloat16 [128, 64, 2880], P('expert', None, 'tensor'), may hold values from -0.75 to 0.75
Outputs:
- mixed: bfloat16 [16384, 2880], P('expert', 'tensor')
The draws below stay inside these ranges and needn't reach their ends.
Inputs may be any that keep to these rules, and one draw needn't show every extreme that they name: `routes`: each row names 4 different experts; among the 128 rows of one block no expert is named more than 5 times, a bound that some expert reaches in some of these blocks.
All inputs are finite; a program needn't handle non-finite values.
Results may differ from the reference program's by a relative error of at most 0.018.
Values may be sent and summed in bfloat16 or wider, within the bound.
A program may use at most 64 MiB of HBM per device.

```python
import math
import jax
import jax.numpy as jnp
import numpy as np
from jax import lax

MODEL_WIDTH = 2880
TOP = 4
HIDDEN_UNITS = 1440
ADAPTER_RANK = 64
TOK_DEV = 128
EXPERT_COUNT = 128
TOKENS = 16384
CAP = 5
N_TENSOR = 4


def touch_ends(array, rng, least, high):
    longest = array.shape.index(max(array.shape))
    spots = []
    for shift in (0, 1):
        where = [jax.random.randint(jax.random.fold_in(rng, axis), (), 0, length) for axis, length in enumerate(array.shape)]
        where[longest] = (where[longest] + shift) % array.shape[longest]
        spots.append(tuple(where))
    return array.at[spots[0]].set(least).at[spots[1]].set(high)


def shard_levels(rng, extent, shards, least, top_value):
    factor_of, own = 1.0, jax.random.fold_in(rng, 6)
    for axis_at, parts in shards:
        draws = jnp.exp(jax.random.uniform(jax.random.fold_in(own, axis_at), (parts,), jnp.float32, least / len(shards), top_value / len(shards)))
        factor_of = factor_of * jnp.repeat(draws, extent[axis_at] // parts).reshape([-1 if axis == axis_at else 1 for axis in range(len(extent))])
    return factor_of


def assign_block(stream_key, own, number, rows, number_of, top, reach, skew):
    ranking = jax.random.permutation(stream_key, number_of)
    crowded, common = shares(number_of, rows * top, reach, skew, True), shares(number_of, rows * top, reach, skew, False)
    places = jnp.arange(number_of)

    def named(tallies, offset_by):
        used = int((tallies > 0).sum())
        fixed = max(1, used // 4)
        moved = fixed + (places - fixed + offset_by * (used - fixed)) % max(1, number_of - fixed)
        return jnp.zeros((number_of,), jnp.int32).at[ranking[jnp.where(places < fixed, places, moved)]].set(jnp.asarray(tallies, jnp.int32))

    tallies = jnp.where(number % 4 == 0, named(crowded, number // 4), named(common, number - number // 4 - 1))
    mixed = jax.random.permutation(jax.random.fold_in(own, 3), number_of)
    source_of, sink = mixed[0:number_of // 2 * 2:2], mixed[1:number_of // 2 * 2:2]
    margin = jnp.minimum(tallies[source_of] - 1, reach - tallies[sink]) // 2
    margin = jnp.where((source_of == ranking[0]) | (sink == ranking[0]) | (tallies[sink] == 0), 0, jnp.maximum(margin, 0))
    moved = jax.random.randint(jax.random.fold_in(own, 4), (number_of // 2,), 0, 1 << 20) % (margin + 1)
    tallies = tallies.at[source_of].add(-moved).at[sink].add(moved)
    labels = jnp.searchsorted(jnp.cumsum(tallies), jnp.arange(rows * top), side="right").astype(jnp.int32)
    listing = labels.reshape(top, rows).T
    listing = listing[jax.random.permutation(jax.random.fold_in(own, 1), rows)]
    offset_by = jax.random.randint(jax.random.fold_in(own, 2), (rows, 1), 0, top)
    return jnp.take_along_axis(listing, (jnp.arange(top)[None, :] + offset_by) % top, axis=1)


def shares(number_of, total, reach, skew, full):
    loads = [(1 << 20) // math.isqrt(rank ** skew) + 1 for rank in range(1, number_of + 1)]
    largest = reach if full else min(reach, max(-(-total // number_of), total * loads[0] // sum(loads)))
    least = 1 if total - largest >= number_of - 1 else 0
    holding, surplus = [largest] + [least] * (number_of - 1), total - largest - least * (number_of - 1)
    while surplus > 0:
        movable = [i for i in range(1, number_of) if holding[i] < largest] or [i for i in range(1, number_of) if holding[i] < reach]
        mass, budget = sum([loads[i] for i in movable]), surplus
        for i in movable:
            addition = min(reach - holding[i], max(1, budget * loads[i] // mass), surplus)
            holding[i] = holding[i] + addition
            surplus = surplus - addition
    return np.array(holding)


def normal_values(own_key, dims, spread, reach, shards=(), held_as=jnp.bfloat16):
    values = jax.random.normal(own_key, dims, jnp.float32) * spread
    if len(shards) > 0:
        values = shard_levels(own_key, dims, shards, -0.22, 0.18) * values
    return jnp.clip(values, min=-reach, max=reach).astype(held_as)


def setup_inputs(seed: int = 0) -> dict:
    streams_of = jax.random.split(jax.random.key(seed), 10)
    tokens = normal_values(streams_of[0], (TOKENS, MODEL_WIDTH), 1.0, 6.0, ((0, 128), (1, 4)))
    routes_keys = jax.random.split(jax.random.fold_in(streams_of[1], 1), TOKENS // TOK_DEV)
    routes_turns = jax.random.permutation(jax.random.fold_in(streams_of[1], 3), TOKENS // TOK_DEV)
    routes = jax.vmap(lambda own, number: assign_block(jax.random.fold_in(streams_of[1], 2), own, number, TOK_DEV, EXPERT_COUNT, TOP, CAP, 1))(routes_keys, routes_turns).reshape((TOKENS, TOP))
    route_gate_weight = touch_ends(jax.random.randint(streams_of[2], (TOKENS, TOP), 1, 65536), jax.random.fold_in(streams_of[2], 1), 1, 65535).astype(jnp.int32)
    up_frozen_matrix = normal_values(streams_of[3], (EXPERT_COUNT, MODEL_WIDTH, HIDDEN_UNITS), MODEL_WIDTH ** -0.5, 0.109375, ((0, 128), (2, 4)))
    down_frozen_matrix = normal_values(streams_of[4], (EXPERT_COUNT, HIDDEN_UNITS, MODEL_WIDTH), HIDDEN_UNITS ** -0.5, 0.15625, ((0, 128), (1, 4)))
    up_adapter_input = normal_values(streams_of[5], (EXPERT_COUNT, MODEL_WIDTH, ADAPTER_RANK), MODEL_WIDTH ** -0.5, 0.109375, ((0, 128), (2, 4)))
    up_adapter_output = normal_values(streams_of[6], (EXPERT_COUNT, ADAPTER_RANK, HIDDEN_UNITS), ADAPTER_RANK ** -0.5, 0.75, ((0, 128), (2, 4)))
    down_adapter_input = normal_values(streams_of[7], (EXPERT_COUNT, HIDDEN_UNITS, ADAPTER_RANK), HIDDEN_UNITS ** -0.5, 0.15625, ((0, 128), (1, 4)))
    down_adapter_output = normal_values(streams_of[8], (EXPERT_COUNT, ADAPTER_RANK, MODEL_WIDTH), ADAPTER_RANK ** -0.5, 0.75, ((0, 128), (2, 4)))
    return {"tokens": tokens, "routes": routes, "route_gate_weight": route_gate_weight, "up_frozen_matrix": up_frozen_matrix, "down_frozen_matrix": down_frozen_matrix, "up_adapter_input": up_adapter_input, "up_adapter_output": up_adapter_output, "down_adapter_input": down_adapter_input, "down_adapter_output": down_adapter_output}


def slot_tables(routes):
    blocks = TOKENS // TOK_DEV
    flat = routes.reshape(blocks, TOK_DEV * TOP).astype(jnp.int32)
    one_hot = (flat[:, :, None] == jnp.arange(EXPERT_COUNT, dtype=jnp.int32)[None, None, :]).astype(jnp.int32)
    earlier = jnp.cumsum(one_hot, axis=1) - one_hot
    position = jnp.sum(earlier * one_hot, axis=2).astype(jnp.int32)
    target = (flat * CAP + position).astype(jnp.int32)
    source = (jnp.arange(blocks, dtype=jnp.int32)[:, None] * TOK_DEV
              + jnp.arange(TOK_DEV * TOP, dtype=jnp.int32)[None, :] // TOP).astype(jnp.int32)
    route_table = jnp.full((blocks, EXPERT_COUNT * CAP), TOKENS, jnp.int32)
    route_table = jax.vmap(lambda row, where, what: row.at[where].set(what))(route_table, target, source)
    route_table = route_table.reshape(blocks, EXPERT_COUNT, CAP).transpose(1, 0, 2).reshape(EXPERT_COUNT, blocks * CAP)
    block_ids = jnp.arange(blocks, dtype=jnp.int32)[:, None]
    lookup = (flat * (blocks * CAP) + block_ids * CAP + position).astype(jnp.int32)
    return route_table, lookup.reshape(TOKENS, TOP)


def reference(tokens, routes, route_gate_weight, up_frozen_matrix, down_frozen_matrix, up_adapter_input, up_adapter_output, down_adapter_input, down_adapter_output):
    route_table, lookup = slot_tables(routes)
    padded = jnp.concatenate([tokens, jnp.zeros((1, MODEL_WIDTH), jnp.bfloat16)], axis=0)
    group = HIDDEN_UNITS // N_TENSOR

    def single_expert(items):
        where, w_up, w_down, a_up, b_up, a_down, b_down = items
        rows = jnp.take(padded, where, axis=0)
        up_projected = jnp.dot(rows, w_up, preferred_element_type=jnp.float32)
        codes_up = jnp.dot(rows, a_up, preferred_element_type=jnp.float32).astype(jnp.bfloat16)
        up_projected = up_projected + 0.5 * jnp.dot(codes_up, b_up, preferred_element_type=jnp.float32)
        hidden_state = (up_projected * jax.nn.sigmoid(1.702 * up_projected)).astype(jnp.bfloat16)
        down_adapter_codes = jnp.dot(hidden_state, a_down, preferred_element_type=jnp.float32).astype(jnp.bfloat16)
        partial_value = jnp.zeros((rows.shape[0], MODEL_WIDTH), jnp.float32)
        for index in range(N_TENSOR):
            piece = jnp.dot(hidden_state[:, index * group:(index + 1) * group],
                            w_down[index * group:(index + 1) * group],
                            preferred_element_type=jnp.float32).astype(jnp.bfloat16)
            piece = lax.optimization_barrier(piece)
            partial_value = partial_value + piece.astype(jnp.float32)
        result = partial_value + 0.5 * jnp.dot(down_adapter_codes, b_down, preferred_element_type=jnp.float32)
        return result.astype(jnp.bfloat16)

    expert_outputs = lax.map(single_expert, (route_table, up_frozen_matrix, down_frozen_matrix, up_adapter_input, up_adapter_output, down_adapter_input, down_adapter_output))
    flat_out = expert_outputs.reshape(-1, MODEL_WIDTH)
    scale = route_gate_weight.astype(jnp.float32) / 65536.0
    total = jnp.zeros((TOKENS, MODEL_WIDTH), jnp.float32)
    for choice_index in range(TOP):
        picked = jnp.take(flat_out, lookup[:, choice_index], axis=0).astype(jnp.float32)
        total = total + scale[:, choice_index][:, None] * picked
    return total.astype(jnp.bfloat16)
```

```python
import functools

import jax
import jax.numpy as jnp
from jax import lax
from jax.experimental import pallas as pl
from jax.experimental.pallas import tpu as pltpu
from jax.sharding import PartitionSpec as P

NZ, NY, NX = 8, 8, 4
CAP = 5
SLOTS = 2 * CAP
LANES = 128
BF16, F32, I32 = jnp.bfloat16, jnp.float32, jnp.int32

NN = (((1,), (0,)), ((), ()))
NT = (((1,), (1,)), ((), ()))
TN = (((0,), (0,)), ((), ()))

(OUT_Y, OUT_Z, OUT_RIGHT, OUT_LEFT, OUT_RIGHT2, OUT_LEFT2, SUM_RIGHT, SUM_LEFT, SUM_RIGHT2, SUM_LEFT2,
 BACK_Z, BACK_Y, MERGE) = range(13)
TOK, META, UP_IN, DOWN_OUT = range(4)


def dot(a, b, dims):
    return lax.dot_general(a, b, dims, preferred_element_type=F32)


def kernel(chunks, routes_ref, gates_ref, tok_ref, wup_hbm, wdn_hbm, aup_ref, bup_ref, adn_ref, bdn_ref, out_ref,
           tok2, meta, sel, ghi, glo, perm, wraw, wdraw, afull, bfull, w1, w2,
           ysend, yrecv, zsend, gath, acc, hid, part, half_l, half_r, full_l, full_r,
           esend, zback, yback, rback, msend, mrecv, own,
           send_sem, recv_sem, send_once, recv_once, local_sem):
    expert, x = lax.axis_index("expert"), lax.axis_index("tensor")
    z, y, core = expert // (2 * NY), (expert // 2) % NY, expert % 2
    right, left, across = (x + 1) % NX, (x + NX - 1) % NX, (x + 2) % NX
    quarter, tokens = tok_ref.shape
    hidden = bup_ref.shape[1]
    rank = bup_ref.shape[0]
    part_rank = aup_ref.shape[0]
    code_at = w1.shape[1] - rank
    ygroup, zgroup = SLOTS * NZ, SLOTS * NY
    rows = ygroup * NY
    half = rows // 2
    last = quarter - (chunks - 1) * LANES

    def at(zz, yy, cc):
        return {"expert": (zz * NY + yy) * 2 + cc}

    sibling = at(z, y, 1 - core)

    def send(src, dst, kind, k, device):
        pltpu.make_async_remote_copy(
            src_ref=src, dst_ref=dst, send_sem=send_sem.at[kind, k], recv_sem=recv_sem.at[kind, k],
            device_id=device, device_id_type=pl.DeviceIdType.MESH).start()

    def arrived(ref, kind, k):
        pltpu.make_async_copy(ref, ref, recv_sem.at[kind, k]).wait()

    def sent(ref, kind, k):
        pltpu.make_async_copy(ref, ref, send_sem.at[kind, k]).wait()

    def send_one(src, dst, which, device):
        pltpu.make_async_remote_copy(
            src_ref=src, dst_ref=dst, send_sem=send_once.at[which], recv_sem=recv_once.at[which],
            device_id=device, device_id_type=pl.DeviceIdType.MESH).start()

    load_up = pltpu.make_async_copy(wup_hbm, wraw, local_sem.at[0])
    load_down = pltpu.make_async_copy(wdn_hbm, wdraw, local_sem.at[1])
    load_up.start()
    load_down.start()

    barrier = pltpu.get_barrier_semaphore()

    def greet(device):
        pl.semaphore_signal(barrier, inc=1, device_id=device, device_id_type=pl.DeviceIdType.MESH)

    greet(sibling)

    @pl.loop(1, NY)
    def _(j):
        greet(at(z, (y + j) % NY, core))

    @pl.loop(1, NZ)
    def _(j):
        greet(at((z + j) % NZ, y, core))

    @pl.loop(1, NX)
    def _(j):
        greet({"tensor": (x + j) % NX})

    meta[0, 0:4, :] = routes_ref[...]
    meta[0, 4:8, :] = gates_ref[...]
    tok2[0:quarter, 0:tokens] = tok_ref[...]
    tok2[quarter:, :] = jnp.zeros_like(tok2[quarter:, :])
    afull[pl.ds(pl.multiple_of(x * part_rank, part_rank), part_rank), :] = aup_ref[...]
    bfull[x] = bdn_ref[...]

    pl.semaphore_wait(barrier, NY + NZ + NX - 2)

    send_one(meta.at[0], meta.at[1], META, sibling)
    send_one(tok_ref, tok2.at[0:quarter, tokens:2 * tokens], TOK, sibling)

    @pl.loop(1, NX)
    def _(j):
        mine = pl.ds(pl.multiple_of(x * part_rank, part_rank), part_rank)
        send_one(aup_ref, afull.at[mine], UP_IN, {"tensor": (x + j) % NX})
        send_one(bdn_ref, bfull.at[x], DOWN_OUT, {"tensor": (x + j) % NX})

    row = lax.broadcasted_iota(I32, (ygroup, rows), 0)
    column = lax.broadcasted_iota(I32, (ygroup, rows), 1)
    for a in range(NY):
        source = (row % NZ) * ygroup + (row // NZ) * NZ + a
        perm[a * ygroup:(a + 1) * ygroup, :] = (column == source).astype(F32).astype(BF16)

    pltpu.make_async_copy(meta.at[0], meta.at[1], recv_once.at[META]).wait()

    before = (lax.broadcasted_iota(I32, (tokens, tokens), 0)
              < lax.broadcasted_iota(I32, (tokens, tokens), 1)).astype(F32).astype(BF16)
    slot_row = lax.broadcasted_iota(I32, (CAP * NZ, tokens), 0)
    for yy in range(NY):
        expert_id = ((slot_row % NZ) * NY + yy) * 2 + core
        picks, gates = [], []
        for src in range(2):
            hit = jnp.zeros((CAP * NZ, tokens), I32)
            gate = jnp.zeros((CAP * NZ, tokens), I32)
            for k in range(4):
                same = meta[src, k:k + 1, :] == expert_id
                hit = jnp.where(same, 1, hit)
                gate = jnp.where(same, meta[src, 4 + k:5 + k, :], gate)
            position = dot(hit.astype(F32).astype(BF16), before, NN)
            pick = jnp.where(position == (slot_row // NZ).astype(F32), hit, 0)
            picks.append(pick)
            gates.append(gate * pick)
        none = jnp.zeros((CAP * NZ, tokens), I32)

        def both(values):
            grid = jnp.concatenate([jnp.concatenate([values[0], none], axis=1),
                                    jnp.concatenate([none, values[1]], axis=1)], axis=0)
            return grid.astype(F32)

        block = slice(yy * ygroup, (yy + 1) * ygroup)
        sel[block, :] = both(picks).astype(BF16)
        ghi[block, :] = (both([g >> 8 for g in gates]) * (1.0 / 256.0)).astype(BF16)
        glo[block, :] = (both([g & 255 for g in gates]) * (1.0 / 65536.0)).astype(BF16)

    pltpu.make_async_copy(tok_ref, tok2.at[0:quarter, tokens:2 * tokens], recv_once.at[TOK]).wait()

    def yblock(j):
        return pl.ds(pl.multiple_of(j * ygroup, 16), ygroup)

    def zblock(j):
        return pl.ds(pl.multiple_of(j * zgroup, 16), zgroup)

    def choose(k):
        feats = pl.ds(pl.multiple_of(k * LANES, LANES), LANES)
        ysend[k] = dot(sel[...], tok2[feats, :], NT).astype(BF16)

        @pl.loop(1, NY)
        def _(j):
            yy = (y + j) % NY
            send(ysend.at[k, yblock(yy)], yrecv.at[k, yblock(y)], OUT_Y, k, at(z, yy, core))

        yrecv[k, yblock(y), :] = ysend[k, yblock(y), :]

    def pass_z(k):
        arrived(yrecv.at[k, 0:rows - ygroup], OUT_Y, k)
        zsend[k] = dot(perm[...], yrecv[k], NN).astype(BF16)

        @pl.loop(1, NZ)
        def _(j):
            zz = (z + j) % NZ
            send(zsend.at[k, zblock(zz)], gath.at[k, x, zblock(z)], OUT_Z, k, at(zz, y, core))

        gath[k, x, zblock(z), :] = zsend[k, zblock(z), :]

    def spread(k):
        arrived(gath.at[k, x, 0:rows - zgroup], OUT_Z, k)
        send(gath.at[k, x], gath.at[k, x], OUT_RIGHT, k, {"tensor": right})
        send(gath.at[k, x], gath.at[k, x], OUT_LEFT, k, {"tensor": left})

    def forward(k):
        arrived(gath.at[k, left], OUT_RIGHT, k)
        send(gath.at[k, left, 0:half], gath.at[k, left, 0:half], OUT_RIGHT2, k, {"tensor": right})
        arrived(gath.at[k, right], OUT_LEFT, k)
        send(gath.at[k, right, half:rows], gath.at[k, right, half:rows], OUT_LEFT2, k, {"tensor": left})

    def multiply(k):
        arrived(gath.at[k, across, 0:half], OUT_RIGHT2, k)
        arrived(gath.at[k, across, half:rows], OUT_LEFT2, k)
        lhs = jnp.concatenate([gath[k, q] for q in range(NX)], axis=1)
        acc[...] += dot(lhs, w1[k], NT)

    def arrange(raw, weights):
        for k in range(chunks):
            width = min(LANES, quarter - k * LANES)
            for q in range(NX):
                first = q * quarter + k * LANES
                weights[k, 0:hidden, q * LANES:q * LANES + width] = raw[0, :, first:first + width]

    def arrange_up():
        load_up.wait()
        w1[...] = jnp.zeros_like(w1)
        arrange(wraw, w1)
        pltpu.make_async_copy(afull.at[0:(NX - 1) * part_rank], afull.at[0:(NX - 1) * part_rank],
                              recv_once.at[UP_IN]).wait()
        for k in range(chunks):
            width = min(LANES, quarter - k * LANES)
            for q in range(NX):
                first = q * quarter + k * LANES
                w1[k, code_at:, q * LANES:q * LANES + width] = afull[:, first:first + width]

    def arrange_down():
        load_down.wait()
        w2[...] = jnp.zeros_like(w2)
        arrange(wdraw, w2)
        pltpu.make_async_copy(bfull.at[0:NX - 1], bfull.at[0:NX - 1], recv_once.at[DOWN_OUT]).wait()
        for k in range(chunks):
            width = min(LANES, quarter - k * LANES)
            for q in range(NX):
                w2[k, code_at:, q * LANES:q * LANES + width] = bfull[q, :, k * LANES:k * LANES + width]

    choose(0)
    choose(1)
    acc[...] = jnp.zeros_like(acc)
    hid[...] = jnp.zeros_like(hid)
    arrange_up()

    def step(tick, stage, delay):
        k = tick - delay

        @pl.when((k >= 0) & (k < chunks))
        def _():
            stage(k)

    @pl.loop(0, chunks + 3)
    def _(t):
        step(t, spread, 1)
        step(t, pass_z, 0)
        step(t, choose, -2)

        @pl.when(t == 0)
        def _():
            arrange_down()

        step(t, forward, 2)
        step(t, multiply, 3)

    codes = acc[:, code_at:].astype(BF16)
    upward = acc[:, 0:hidden] + 0.5 * dot(codes, bup_ref[...], NN)
    units = (upward * jax.nn.sigmoid(1.702 * upward)).astype(BF16)
    hid[:, 0:hidden] = units
    hid[:, code_at:] = (0.5 * dot(units, adn_ref[...], NT)).astype(BF16)

    def partial(k):
        product = dot(hid[...], w2[k], NN).astype(BF16)
        for q in range(NX):
            part[k, q] = product[:, q * LANES:(q + 1) * LANES]
        send(part.at[k, across, 0:half], half_l.at[k], SUM_RIGHT, k, {"tensor": right})
        send(part.at[k, across, half:rows], half_r.at[k], SUM_LEFT, k, {"tensor": left})

    def add_half(k):
        arrived(half_l.at[k], SUM_RIGHT, k)
        part[k, right, 0:half, :] = (part[k, right, 0:half, :].astype(F32) + half_l[k].astype(F32)).astype(BF16)
        send(part.at[k, right], full_l.at[k], SUM_RIGHT2, k, {"tensor": right})
        arrived(half_r.at[k], SUM_LEFT, k)
        part[k, left, half:rows, :] = (part[k, left, half:rows, :].astype(F32) + half_r[k].astype(F32)).astype(BF16)
        send(part.at[k, left], full_r.at[k], SUM_LEFT2, k, {"tensor": left})

    def add_full(k):
        arrived(full_l.at[k], SUM_RIGHT2, k)
        arrived(full_r.at[k], SUM_LEFT2, k)
        total = part[k, x].astype(F32) + full_l[k].astype(F32) + full_r[k].astype(F32)
        esend[k] = total.astype(BF16)

        @pl.loop(1, NZ)
        def _(j):
            zz = (z + j) % NZ
            send(esend.at[k, zblock(zz)], zback.at[k, zblock(z)], BACK_Z, k, at(zz, y, core))

        zback[k, zblock(z), :] = esend[k, zblock(z), :]

    def pass_y(k):
        arrived(zback.at[k, 0:rows - zgroup], BACK_Z, k)
        yback[k] = dot(perm[...], zback[k], NN).astype(BF16)

        @pl.loop(1, NY)
        def _(j):
            yy = (y + j) % NY
            send(yback.at[k, yblock(yy)], rback.at[k, yblock(y)], BACK_Y, k, at(z, yy, core))

        rback[k, yblock(y), :] = yback[k, yblock(y), :]

    def mix(k):
        arrived(rback.at[k, 0:rows - ygroup], BACK_Y, k)
        mixed = dot(rback[k], ghi[...], TN) + dot(rback[k], glo[...], TN)
        own[k] = mixed[:, 0:tokens]
        msend[k] = mixed[:, tokens:]
        send(msend.at[k], mrecv.at[k], MERGE, k, sibling)

    @pl.loop(0, chunks + 4)
    def _(t):
        step(t, add_full, 2)
        step(t, partial, 0)
        step(t, add_half, 1)
        step(t, pass_y, 3)
        step(t, mix, 4)

    for k in range(chunks):
        width = min(LANES, quarter - k * LANES)
        arrived(mrecv.at[k], MERGE, k)
        out_ref[k * LANES:k * LANES + width, :] = (own[k, 0:width, :] + mrecv[k, 0:width, :]).astype(BF16)

    @pl.loop(0, chunks)
    def _(k):
        sent(ysend.at[k, 0:rows - ygroup], OUT_Y, k)
        sent(zsend.at[k, 0:rows - zgroup], OUT_Z, k)
        sent(gath.at[k, 0], OUT_RIGHT, k)
        sent(gath.at[k, 0], OUT_LEFT, k)
        sent(gath.at[k, 0, 0:half], OUT_RIGHT2, k)
        sent(gath.at[k, 0, 0:half], OUT_LEFT2, k)
        sent(half_l.at[k], SUM_RIGHT, k)
        sent(half_r.at[k], SUM_LEFT, k)
        sent(full_l.at[k], SUM_RIGHT2, k)
        sent(full_r.at[k], SUM_LEFT2, k)
        sent(esend.at[k, 0:rows - zgroup], BACK_Z, k)
        sent(yback.at[k, 0:rows - ygroup], BACK_Y, k)
        sent(msend.at[k], MERGE, k)

    pltpu.make_async_copy(meta.at[0], meta.at[1], send_once.at[META]).wait()
    pltpu.make_async_copy(tok_ref, tok2.at[0:quarter, tokens:2 * tokens], send_once.at[TOK]).wait()
    pltpu.make_async_copy(afull.at[0:(NX - 1) * part_rank], afull.at[0:(NX - 1) * part_rank],
                          send_once.at[UP_IN]).wait()
    pltpu.make_async_copy(bfull.at[0:NX - 1], bfull.at[0:NX - 1], send_once.at[DOWN_OUT]).wait()


def local(tokens, routes, gates, wup, wdn, aup, bup, adn, bdn):
    count, quarter = tokens.shape
    hidden, rank = wup.shape[2], bup.shape[1]
    part_rank = aup.shape[2]
    chunks = -(-quarter // LANES)
    rows = SLOTS * NY * NZ
    inner = -(-hidden // LANES) * LANES + rank
    grid = (chunks, rows, LANES)
    vmem, hbm = pl.BlockSpec(memory_space=pltpu.VMEM), pl.BlockSpec(memory_space=pl.ANY)
    out = pl.pallas_call(
        functools.partial(kernel, chunks),
        out_shape=jax.ShapeDtypeStruct((quarter, count), BF16),
        in_specs=[vmem, vmem, vmem, hbm, hbm, vmem, vmem, vmem, vmem],
        out_specs=vmem,
        scratch_shapes=[
            pltpu.VMEM((chunks * LANES, 2 * count), BF16),
            pltpu.VMEM((2, 8, count), I32),
            pltpu.VMEM((rows, 2 * count), BF16),
            pltpu.VMEM((rows, 2 * count), BF16),
            pltpu.VMEM((rows, 2 * count), BF16),
            pltpu.VMEM((rows, rows), BF16),
            pltpu.VMEM((1, hidden, NX * quarter), BF16),
            pltpu.VMEM((1, hidden, NX * quarter), BF16),
            pltpu.VMEM((rank, NX * quarter), BF16),
            pltpu.VMEM((NX, rank, quarter), BF16),
            pltpu.VMEM((chunks, inner, NX * LANES), BF16),
            pltpu.VMEM((chunks, inner, NX * LANES), BF16),
            pltpu.VMEM(grid, BF16),
            pltpu.VMEM(grid, BF16),
            pltpu.VMEM(grid, BF16),
            pltpu.VMEM((chunks, NX, rows, LANES), BF16),
            pltpu.VMEM((rows, inner), F32),
            pltpu.VMEM((rows, inner), BF16),
            pltpu.VMEM((chunks, NX, rows, LANES), BF16),
            pltpu.VMEM((chunks, rows // 2, LANES), BF16),
            pltpu.VMEM((chunks, rows // 2, LANES), BF16),
            pltpu.VMEM(grid, BF16),
            pltpu.VMEM(grid, BF16),
            pltpu.VMEM(grid, BF16),
            pltpu.VMEM(grid, BF16),
            pltpu.VMEM(grid, BF16),
            pltpu.VMEM(grid, BF16),
            pltpu.VMEM((chunks, LANES, count), F32),
            pltpu.VMEM((chunks, LANES, count), F32),
            pltpu.VMEM((chunks, LANES, count), F32),
            pltpu.SemaphoreType.DMA((13, chunks)),
            pltpu.SemaphoreType.DMA((13, chunks)),
            pltpu.SemaphoreType.DMA((4,)),
            pltpu.SemaphoreType.DMA((4,)),
            pltpu.SemaphoreType.DMA((2,)),
        ],
        compiler_params=pltpu.CompilerParams(
            collective_id=0, has_side_effects=True, vmem_limit_bytes=50 * 1024 * 1024),
        cost_estimate=pl.CostEstimate(flops=8 * 10**9, bytes_accessed=6 * 10**6, transcendentals=0),
    )(routes.T, gates.T, tokens.T, jnp.swapaxes(wup, 1, 2), wdn, aup[0].T, bup[0], adn[0].T, bdn[0])
    return out.T


def solution(mesh):
    return jax.shard_map(
        local,
        mesh=mesh,
        in_specs=(
            P("expert", "tensor"),
            P("expert", None),
            P("expert", None),
            P("expert", None, "tensor"),
            P("expert", "tensor", None),
            P("expert", None, "tensor"),
            P("expert", None, "tensor"),
            P("expert", "tensor", None),
            P("expert", None, "tensor"),
        ),
        out_specs=P("expert", "tensor"),
        check_vma=False,
    )
```

```python
import functools

import jax
import jax.numpy as jnp
from jax import lax
from jax.experimental import pallas as pl
from jax.experimental.pallas import tpu as pltpu
from jax.sharding import PartitionSpec as P

NZ, NY, NX = 8, 8, 4
CAP = 5
SLOTS = 2 * CAP
LANES = 128
BF16, F32, I32 = jnp.bfloat16, jnp.float32, jnp.int32

NN = (((1,), (0,)), ((), ()))
NT = (((1,), (1,)), ((), ()))
TN = (((0,), (0,)), ((), ()))

(OUT_1, OUT_2, OUT_RIGHT, OUT_LEFT, OUT_RIGHT2, OUT_LEFT2, SUM_RIGHT, SUM_LEFT, SUM_RIGHT2, SUM_LEFT2,
 BACK_1, BACK_2, MERGE, KINDS) = range(14)
TOK, META, UP_IN, DOWN_OUT = range(4)


def dot(a, b, dims):
    return lax.dot_general(a, b, dims, preferred_element_type=F32)


def kernel(chunks, routes_hbm, gates_hbm, tok_hbm, wup_hbm, wdn_hbm, aup_hbm, bup_hbm, adn_hbm, bdn_hbm, out_ref,
           routes_ref, gates_ref, tok_ref, aup_ref, bup_ref, adn_ref, bdn_ref, tok2, meta, sel, selz, gain, gainz, perm, wraw, wdraw, afull, bfull, w1, w2,
           ysend, yrecv, zsend, late, gath, acc, hid, part, half_l, half_r, full_l, full_r,
           total, esend, zback, yback, rback, msend, mrecv, own,
           send_sem, recv_sem, send_once, recv_once, local_sem):
    expert, x = lax.axis_index("expert"), lax.axis_index("tensor")
    z, y, core = expert // (2 * NY), (expert // 2) % NY, expert % 2
    right, left, across = (x + 1) % NX, (x + NX - 1) % NX, (x + 2) % NX
    quarter, tokens = tok_ref.shape
    hidden = bup_ref.shape[1]
    rank = bup_ref.shape[0]
    part_rank = aup_ref.shape[0]
    code_at = w1.shape[1] - rank
    ygroup = SLOTS * NZ
    rows = ygroup * NY
    half = rows // 2
    last = quarter - (chunks - 1) * LANES

    def at(zz, yy, cc):
        return {"expert": (zz * NY + yy) * 2 + cc}

    sibling = at(z, y, 1 - core)

    def send(src, dst, kind, k, device):
        pltpu.make_async_remote_copy(
            src_ref=src, dst_ref=dst, send_sem=send_sem.at[kind, k], recv_sem=recv_sem.at[kind, k],
            device_id=device, device_id_type=pl.DeviceIdType.MESH).start()

    def arrived(ref, kind, k):
        pltpu.make_async_copy(ref, ref, recv_sem.at[kind, k]).wait()

    def sent(ref, kind, k):
        pltpu.make_async_copy(ref, ref, send_sem.at[kind, k]).wait()

    def send_one(src, dst, which, device):
        pltpu.make_async_remote_copy(
            src_ref=src, dst_ref=dst, send_sem=send_once.at[which], recv_sem=recv_once.at[which],
            device_id=device, device_id_type=pl.DeviceIdType.MESH).start()

    loads = [pltpu.make_async_copy(hbm, ref, local_sem.at[i]) for i, (hbm, ref) in enumerate((
        (routes_hbm, routes_ref), (gates_hbm, gates_ref), (tok_hbm, tok_ref), (aup_hbm, aup_ref), (bdn_hbm, bdn_ref),
        (wup_hbm, wraw), (wdn_hbm, wdraw), (bup_hbm, bup_ref), (adn_hbm, adn_ref)))]
    for load in loads:
        load.start()
    load_up, load_down, load_bup, load_adn = loads[5:]

    barrier = pltpu.get_barrier_semaphore()

    def greet(device):
        pl.semaphore_signal(barrier, inc=1, device_id=device, device_id_type=pl.DeviceIdType.MESH)

    greet(sibling)

    @pl.loop(1, NY)
    def _(j):
        greet(at(z, (y + j) % NY, core))

    @pl.loop(1, NZ)
    def _(j):
        greet(at((z + j) % NZ, y, core))

    @pl.loop(1, NX)
    def _(j):
        greet({"tensor": (x + j) % NX})

    for load in loads[:2]:
        load.wait()
    meta[0, 0:4, :] = routes_ref[...]
    meta[0, 4:8, :] = gates_ref[...]

    before = (lax.broadcasted_iota(I32, (tokens, tokens), 0)
              < lax.broadcasted_iota(I32, (tokens, tokens), 1)).astype(F32).astype(BF16)
    slot_row = lax.broadcasted_iota(I32, (CAP * NZ, tokens), 0)
    slot_of = (slot_row // NZ).astype(F32)
    first_id = (slot_row % NZ) * (2 * NY) + core
    none = jnp.zeros((CAP * NZ, tokens), F32)

    def picks(src):
        for yy in range(NY):
            hit = jnp.zeros((CAP * NZ, tokens), F32)
            for k in range(4):
                hit = jnp.where(meta[src, k:k + 1, :] == first_id + 2 * yy, 1.0, hit)
            position = dot(hit.astype(BF16), before, NN)
            yield jnp.where(position == slot_of, hit, 0.0)

    def both(mine, theirs):
        return jnp.concatenate([jnp.concatenate([mine, none], axis=1),
                                jnp.concatenate([none, theirs], axis=1)], axis=0).astype(BF16)

    row = lax.broadcasted_iota(I32, (ygroup, rows), 0)
    column = lax.broadcasted_iota(I32, (ygroup, rows), 1)
    source = (row % NZ) * ygroup + (row // NZ) * NZ
    for a in range(NY):
        perm[a * ygroup:(a + 1) * ygroup, :] = (column == source + a).astype(F32).astype(BF16)
    own_picks = list(picks(0))
    for load in loads[2:5]:
        load.wait()

    pl.semaphore_wait(barrier, NY + NZ + NX - 2)

    send_one(meta.at[0], meta.at[1], META, sibling)
    send_one(tok_ref, tok2.at[0:quarter, tokens:2 * tokens], TOK, sibling)

    @pl.loop(1, NX)
    def _(j):
        mine = pl.ds(pl.multiple_of(x * part_rank, part_rank), part_rank)
        send_one(aup_ref, afull.at[mine], UP_IN, {"tensor": (x + j) % NX})
        send_one(bdn_ref, bfull.at[x], DOWN_OUT, {"tensor": (x + j) % NX})

    tok2[0:quarter, 0:tokens] = tok_ref[...]
    tok2[quarter:, :] = jnp.zeros_like(tok2[quarter:, :])

    pltpu.make_async_copy(meta.at[0], meta.at[1], recv_once.at[META]).wait()
    for yy, (mine, theirs) in enumerate(zip(own_picks, picks(1))):
        sel[yy * ygroup:(yy + 1) * ygroup, :] = both(mine, theirs)

    def prepare():
        acc[...] = jnp.zeros_like(acc)
        hid[...] = jnp.zeros_like(hid)
        afull[pl.ds(pl.multiple_of(x * part_rank, part_rank), part_rank), :] = aup_ref[...]
        bfull[x] = bdn_ref[...]

    def weigh():
        for yy in range(NY):
            block = slice(yy * ygroup, (yy + 1) * ygroup)
            highs, lows = [], []
            for src in range(2):
                gate = jnp.zeros((CAP * NZ, tokens), I32)
                for k in range(4):
                    same = meta[src, k:k + 1, :] == first_id + 2 * yy
                    gate = jnp.where(same, meta[src, 4 + k:5 + k, :], gate)
                highs.append((gate >> 8).astype(F32) * (1.0 / 256.0))
                lows.append((gate & 255).astype(F32) * (1.0 / 65536.0))
            pick = sel[block, :]
            gain[block, 0:2 * tokens] = pick * both(*highs)
            gain[block, 2 * tokens:] = pick * both(*lows)
        gainz[...] = dot(perm[...], gain[...], NN).astype(BF16)

    pltpu.make_async_copy(tok_ref, tok2.at[0:quarter, tokens:2 * tokens], recv_once.at[TOK]).wait()

    place = (y, z)

    def block(i):
        return pl.ds(pl.multiple_of(i * ygroup, 16), ygroup)

    def scatter(src, dst, axis, kind, k):
        @pl.loop(1, NY)
        def _(j):
            i = (place[axis] + j) % NY
            send(src.at[block(i)], dst.at[block(place[axis])], kind, k, at(z, i, core) if axis == 0 else at(i, y, core))

        dst[block(place[axis]), :] = src[block(place[axis]), :]

    def choose(k, p):
        feats = pl.ds(pl.multiple_of(k * LANES, LANES), LANES)
        ysend[k] = dot((sel, selz)[p][...], tok2[feats, :], NT).astype(BF16)
        scatter(ysend.at[k], yrecv.at[k], p, OUT_1, k)

    def pass_on(k, p):
        arrived(yrecv.at[k, 0:rows - ygroup], OUT_1, k)
        zsend[k] = dot(perm[...], yrecv[k], NN).astype(BF16)
        scatter(zsend.at[k], late.at[k] if p else gath.at[k, x], 1 - p, OUT_2, k)

    def span(h, scale=1):
        count = rows // scale
        return slice(0, count) if h is None else slice(h * count // 2, (h + 1) * count // 2)

    def slot(k, h):
        return k + chunks if h == 1 else k

    def ends(h):
        whole = span(h)
        middle = (whole.start + whole.stop) // 2
        return slice(whole.start, middle), slice(middle, whole.stop)

    def spread(k, p, h=None):
        if h != 1:
            arrived(yrecv.at[k, 0:rows - ygroup], OUT_2, k)
            if p:
                gath[k, x] = dot(perm[...], late[k], NN).astype(BF16)
        mine = gath.at[k, x, span(h)]
        send(mine, mine, OUT_RIGHT, slot(k, h), {"tensor": right})
        send(mine, mine, OUT_LEFT, slot(k, h), {"tensor": left})

    def forward(k, h=None):
        top, bottom = ends(h)
        arrived(gath.at[k, left, span(h)], OUT_RIGHT, slot(k, h))
        send(gath.at[k, left, top], gath.at[k, left, top], OUT_RIGHT2, slot(k, h), {"tensor": right})
        arrived(gath.at[k, right, span(h)], OUT_LEFT, slot(k, h))
        send(gath.at[k, right, bottom], gath.at[k, right, bottom], OUT_LEFT2, slot(k, h), {"tensor": left})

    def multiply(k, h=None):
        top, bottom = ends(h)
        arrived(gath.at[k, across, top], OUT_RIGHT2, slot(k, h))
        arrived(gath.at[k, across, bottom], OUT_LEFT2, slot(k, h))
        lhs = jnp.concatenate([gath[k, q, span(h), :] for q in range(NX)], axis=1)
        acc[span(h), :] += dot(lhs, w1[k], NT)

    def arrange(raw, weights):
        for k in range(chunks):
            width = min(LANES, quarter - k * LANES)
            for q in range(NX):
                first = q * quarter + k * LANES
                weights[k, 0:hidden, q * LANES:q * LANES + width] = raw[0, :, first:first + width]

    def arrange_up():
        load_up.wait()
        w1[...] = jnp.zeros_like(w1)
        arrange(wraw, w1)

    def arrange_down():
        load_down.wait()
        w2[...] = jnp.zeros_like(w2)
        arrange(wdraw, w2)

    def arrange_adapters():
        pltpu.make_async_copy(afull.at[0:(NX - 1) * part_rank], afull.at[0:(NX - 1) * part_rank],
                              recv_once.at[UP_IN]).wait()
        pltpu.make_async_copy(bfull.at[0:NX - 1], bfull.at[0:NX - 1], recv_once.at[DOWN_OUT]).wait()
        for k in range(chunks):
            width = min(LANES, quarter - k * LANES)
            for q in range(NX):
                first = q * quarter + k * LANES
                w1[k, code_at:, q * LANES:q * LANES + width] = afull[:, first:first + width]
                w2[k, code_at:, q * LANES:q * LANES + width] = bfull[q, :, k * LANES:k * LANES + width]

    pairs = chunks // 2

    def step(tick, stage, delay, parity, *more):
        pair = tick - delay

        @pl.when((pair >= 0) & (pair < pairs))
        def _():
            stage(2 * pair + parity, *more)

    choose(0, 0)
    selz[...] = dot(perm[...], sel[...], NN).astype(BF16)
    choose(1, 1)
    if pairs > 1:
        choose(2, 0)
        choose(3, 1)
    prepare()
    arrange_up()

    @pl.loop(0, pairs)
    def _(t):
        step(t, pass_on, 0, 0, 0)
        step(t, pass_on, 0, 1, 1)
        step(t, choose, -2, 0, 0)
        step(t, choose, -2, 1, 1)

        @pl.when(t == 0)
        def _():
            weigh()

        step(t, forward, 2, 0)
        step(t, spread, 1, 0, 0)
        step(t, spread, 1, 1, 1)

        @pl.when(t == min(1, pairs - 1))
        def _():
            arrange_down()
            arrange_adapters()

        step(t, forward, 2, 1)
        step(t, multiply, 3, 1)
        step(t, multiply, 2, 0)

    load_bup.wait()
    load_adn.wait()

    def activate(h):
        codes = acc[span(h), code_at:].astype(BF16)
        upward = acc[span(h), 0:hidden] + 0.5 * dot(codes, bup_ref[...], NN)
        units = (upward * jax.nn.sigmoid(1.702 * upward)).astype(BF16)
        hid[span(h), 0:hidden] = units
        hid[span(h), code_at:] = (0.5 * dot(units, adn_ref[...], NT)).astype(BF16)

    def partial(k, h=None):
        top, bottom = ends(h)
        product = dot(hid[span(h), :], w2[k], NN).astype(BF16)
        for q in range(NX):
            part[k, q, span(h), :] = product[:, q * LANES:(q + 1) * LANES]
        send(part.at[k, across, top], half_l.at[k, span(h, 2)], SUM_RIGHT, slot(k, h), {"tensor": right})
        send(part.at[k, across, bottom], half_r.at[k, span(h, 2)], SUM_LEFT, slot(k, h), {"tensor": left})

    def add_half(k, h=None):
        top, bottom = ends(h)
        half_of = span(h, 2)
        arrived(half_l.at[k, half_of], SUM_RIGHT, slot(k, h))
        part[k, right, top, :] = (part[k, right, top, :].astype(F32) + half_l[k, half_of, :].astype(F32)).astype(BF16)
        send(part.at[k, right, span(h)], full_l.at[k, span(h)], SUM_RIGHT2, slot(k, h), {"tensor": right})
        arrived(half_r.at[k, half_of], SUM_LEFT, slot(k, h))
        part[k, left, bottom, :] = (part[k, left, bottom, :].astype(F32)
                                    + half_r[k, half_of, :].astype(F32)).astype(BF16)
        send(part.at[k, left, span(h)], full_r.at[k, span(h)], SUM_LEFT2, slot(k, h), {"tensor": left})

    def add_full(k, p, h=None):
        where = span(h)
        arrived(full_l.at[k, where], SUM_RIGHT2, slot(k, h))
        arrived(full_r.at[k, where], SUM_LEFT2, slot(k, h))
        total[where, :] = (part[k, x, where, :].astype(F32) + full_l[k, where, :].astype(F32)
                           + full_r[k, where, :].astype(F32)).astype(BF16)
        if h != 0:
            esend[k] = dot(perm[...], total[...], NN).astype(BF16) if p else total[...]
            scatter(esend.at[k], zback.at[k], 1 - p, BACK_1, k)

    def pass_back(k, p):
        arrived(zback.at[k, 0:rows - ygroup], BACK_1, k)
        yback[k] = dot(perm[...], zback[k], NN).astype(BF16)
        scatter(yback.at[k], rback.at[k], p, BACK_2, k)

    def mix(k, p):
        arrived(rback.at[k, 0:rows - ygroup], BACK_2, k)
        both_parts = dot(rback[k], (gain, gainz)[p][...], TN)
        mixed = both_parts[:, 0:2 * tokens] + both_parts[:, 2 * tokens:]
        own[k] = mixed[:, 0:tokens]
        msend[k] = mixed[:, tokens:]
        send(msend.at[k], mrecv.at[k], MERGE, k, sibling)

    def finish(k):
        arrived(mrecv.at[k], MERGE, k)
        own[k] = own[k] + mrecv[k]

    end = chunks - 2
    more = pairs > 1
    if more:
        forward(end - 2)
    spread(end, 0, 0)
    spread(end + 1, 1, 0)
    if more:
        forward(end - 1)
    spread(end, 0, 1)
    spread(end + 1, 1, 1)
    if pairs > 2:
        multiply(end - 3)
    if more:
        multiply(end - 2)
    forward(end, 0)
    forward(end + 1, 0)
    if more:
        multiply(end - 1)
    forward(end, 1)
    forward(end + 1, 1)
    for h in range(2):
        multiply(end, h)
        multiply(end + 1, h)
        activate(h)
        partial(0, h)
        partial(1, h)
    for h in range(2):
        add_half(0, h)
        add_half(1, h)
        if more:
            partial(2 + h)
    if more:
        add_half(2)
        if pairs > 2:
            partial(4)
    add_full(0, 0, 0)
    add_full(0, 0, 1)
    if more:
        add_half(3)
        if pairs > 2:
            partial(5)
    add_full(1, 1, 0)
    add_full(1, 1, 1)

    @pl.loop(2, pairs + 4)
    def _(t):
        for p in range(2):
            step(t, add_half, 0, p)
            step(t, partial, -1, p)
            step(t, add_full, 1, p, p)
        step(t, pass_back, 2, 0, 0)
        step(t, pass_back, 2, 1, 1)
        step(t, mix, 3, 0, 0)
        step(t, mix, 3, 1, 1)
        step(t, finish, 4, 0)
        step(t, finish, 4, 1)

    for k in range(chunks):
        width = min(LANES, quarter - k * LANES)
        out_ref[k * LANES:k * LANES + width, :] = own[k, 0:width, :].astype(BF16)

    @pl.loop(0, chunks)
    def _(k):
        sent(ysend.at[k, 0:rows - ygroup], OUT_1, k)
        sent(zsend.at[k, 0:rows - ygroup], OUT_2, k)
        sent(esend.at[k, 0:rows - ygroup], BACK_1, k)
        sent(yback.at[k, 0:rows - ygroup], BACK_2, k)
        sent(msend.at[k], MERGE, k)

    for k in range(chunks):
        for h in (0, 1) if k >= end else (None,):
            top, bottom = ends(h)
            sent(gath.at[k, 0, span(h)], OUT_RIGHT, slot(k, h))
            sent(gath.at[k, 0, span(h)], OUT_LEFT, slot(k, h))
            sent(gath.at[k, 0, top], OUT_RIGHT2, slot(k, h))
            sent(gath.at[k, 0, bottom], OUT_LEFT2, slot(k, h))
        for h in (0, 1) if k < 2 else (None,):
            sent(half_l.at[k, span(h, 2)], SUM_RIGHT, slot(k, h))
            sent(half_r.at[k, span(h, 2)], SUM_LEFT, slot(k, h))
            sent(full_l.at[k, span(h)], SUM_RIGHT2, slot(k, h))
            sent(full_r.at[k, span(h)], SUM_LEFT2, slot(k, h))

    pltpu.make_async_copy(meta.at[0], meta.at[1], send_once.at[META]).wait()
    pltpu.make_async_copy(tok_ref, tok2.at[0:quarter, tokens:2 * tokens], send_once.at[TOK]).wait()
    pltpu.make_async_copy(afull.at[0:(NX - 1) * part_rank], afull.at[0:(NX - 1) * part_rank],
                          send_once.at[UP_IN]).wait()
    pltpu.make_async_copy(bfull.at[0:NX - 1], bfull.at[0:NX - 1], send_once.at[DOWN_OUT]).wait()


def local(tokens, routes, gates, wup, wdn, aup, bup, adn, bdn):
    count, quarter = tokens.shape
    hidden, rank = wup.shape[2], bup.shape[1]
    part_rank = aup.shape[2]
    chunks = -(-quarter // LANES)
    rows = SLOTS * NY * NZ
    inner = -(-hidden // LANES) * LANES + rank
    grid = (chunks, rows, LANES)
    vmem, hbm = pl.BlockSpec(memory_space=pltpu.VMEM), pl.BlockSpec(memory_space=pl.ANY)
    out = pl.pallas_call(
        functools.partial(kernel, chunks),
        out_shape=jax.ShapeDtypeStruct((quarter, count), BF16),
        in_specs=[hbm] * 9,
        out_specs=vmem,
        scratch_shapes=[
            pltpu.VMEM((4, count), I32),
            pltpu.VMEM((4, count), I32),
            pltpu.VMEM((quarter, count), BF16),
            pltpu.VMEM((part_rank, NX * quarter), BF16),
            pltpu.VMEM((rank, hidden), BF16),
            pltpu.VMEM((rank, hidden), BF16),
            pltpu.VMEM((rank, quarter), BF16),
            pltpu.VMEM((chunks * LANES, 2 * count), BF16),
            pltpu.VMEM((2, 8, count), I32),
            pltpu.VMEM((rows, 2 * count), BF16),
            pltpu.VMEM((rows, 2 * count), BF16),
            pltpu.VMEM((rows, 4 * count), BF16),
            pltpu.VMEM((rows, 4 * count), BF16),
            pltpu.VMEM((rows, rows), BF16),
            pltpu.VMEM((1, hidden, NX * quarter), BF16),
            pltpu.VMEM((1, hidden, NX * quarter), BF16),
            pltpu.VMEM((rank, NX * quarter), BF16),
            pltpu.VMEM((NX, rank, quarter), BF16),
            pltpu.VMEM((chunks, inner, NX * LANES), BF16),
            pltpu.VMEM((chunks, inner, NX * LANES), BF16),
            pltpu.VMEM(grid, BF16),
            pltpu.VMEM(grid, BF16),
            pltpu.VMEM(grid, BF16),
            pltpu.VMEM(grid, BF16),
            pltpu.VMEM((chunks, NX, rows, LANES), BF16),
            pltpu.VMEM((rows, inner), F32),
            pltpu.VMEM((rows, inner), BF16),
            pltpu.VMEM((chunks, NX, rows, LANES), BF16),
            pltpu.VMEM((chunks, rows // 2, LANES), BF16),
            pltpu.VMEM((chunks, rows // 2, LANES), BF16),
            pltpu.VMEM(grid, BF16),
            pltpu.VMEM(grid, BF16),
            pltpu.VMEM((rows, LANES), BF16),
            pltpu.VMEM(grid, BF16),
            pltpu.VMEM(grid, BF16),
            pltpu.VMEM(grid, BF16),
            pltpu.VMEM(grid, BF16),
            pltpu.VMEM((chunks, LANES, count), F32),
            pltpu.VMEM((chunks, LANES, count), F32),
            pltpu.VMEM((chunks, LANES, count), F32),
            pltpu.SemaphoreType.DMA((KINDS, 2 * chunks)),
            pltpu.SemaphoreType.DMA((KINDS, 2 * chunks)),
            pltpu.SemaphoreType.DMA((4,)),
            pltpu.SemaphoreType.DMA((4,)),
            pltpu.SemaphoreType.DMA((9,)),
        ],
        compiler_params=pltpu.CompilerParams(
            collective_id=0, has_side_effects=True, vmem_limit_bytes=60 * 1024 * 1024),
        cost_estimate=pl.CostEstimate(flops=8 * 10**9, bytes_accessed=6 * 10**6, transcendentals=0),
    )(routes.T, gates.T, tokens.T, jnp.swapaxes(wup, 1, 2), wdn, aup[0].T, bup[0], adn[0].T, bdn[0])
    return out.T


def solution(mesh):
    return jax.shard_map(
        local,
        mesh=mesh,
        in_specs=(
            P("expert", "tensor"),
            P("expert", None),
            P("expert", None),
            P("expert", None, "tensor"),
            P("expert", "tensor", None),
            P("expert", None, "tensor"),
            P("expert", None, "tensor"),
            P("expert", "tensor", None),
            P("expert", None, "tensor"),
        ),
        out_specs=P("expert", "tensor"),
        check_vma=False,
    )
```

```python
import functools

import jax
import jax.numpy as jnp
from jax import lax
from jax.experimental import pallas as pl
from jax.experimental.pallas import tpu as pltpu
from jax.sharding import PartitionSpec as P

NZ, NY, NX = 8, 8, 4
CAP = 5
SLOTS = 2 * CAP
LANES = 128
BF16, F32, I32 = jnp.bfloat16, jnp.float32, jnp.int32

NN = (((1,), (0,)), ((), ()))
NT = (((1,), (1,)), ((), ()))
TN = (((0,), (0,)), ((), ()))

(OUT_1, OUT_2, OUT_RIGHT, OUT_LEFT, OUT_RIGHT2, OUT_LEFT2, SUM_RIGHT, SUM_LEFT, SUM_RIGHT2, SUM_LEFT2,
 BACK_1, BACK_2, KINDS) = range(13)
UP_IN, DOWN_OUT = range(2)


def dot(a, b, dims):
    return lax.dot_general(a, b, dims, preferred_element_type=F32)


def kernel(chunks, routes_hbm, gates_hbm, tok_hbm, wup_hbm, wdn_hbm, aup_hbm, bup_hbm, adn_hbm, bdn_hbm, out_ref,
           routes_ref, gates_ref, tok_ref, aup_ref, bup_ref, adn_ref, bdn_ref, tok2, sel, selz, gain, gainz, perm, merge, split, wraw, wdraw, afull, bfull, w1, w2,
           ysend, yrecv, zsend, late, gath, acc, hid, part, half_l, half_r, full_l, full_r,
           total, esend, zback, yback, rback, own,
           send_sem, recv_sem, send_once, recv_once, local_sem):
    expert, x = lax.axis_index("expert"), lax.axis_index("tensor")
    z, y, core = expert // (2 * NY), (expert // 2) % NY, expert % 2
    right, left, across = (x + 1) % NX, (x + NX - 1) % NX, (x + 2) % NX
    quarter, tokens = tok_ref.shape
    hidden = bup_ref.shape[1]
    rank = bup_ref.shape[0]
    part_rank = aup_ref.shape[0]
    code_at = w1.shape[1] - rank
    ygroup = SLOTS * NZ
    rows = ygroup * NY
    half = rows // 2
    filled = CAP * NZ
    padded = -(-filled // 16) * 16
    spread_rows = 2 * NY * padded
    last = quarter - (chunks - 1) * LANES

    def at(zz, yy, cc):
        return {"expert": (zz * NY + yy) * 2 + cc}

    def send(src, dst, kind, k, device):
        pltpu.make_async_remote_copy(
            src_ref=src, dst_ref=dst, send_sem=send_sem.at[kind, k], recv_sem=recv_sem.at[kind, k],
            device_id=device, device_id_type=pl.DeviceIdType.MESH).start()

    def arrived(ref, kind, k):
        pltpu.make_async_copy(ref, ref, recv_sem.at[kind, k]).wait()

    def sent(ref, kind, k):
        pltpu.make_async_copy(ref, ref, send_sem.at[kind, k]).wait()

    def send_one(src, dst, which, device):
        pltpu.make_async_remote_copy(
            src_ref=src, dst_ref=dst, send_sem=send_once.at[which], recv_sem=recv_once.at[which],
            device_id=device, device_id_type=pl.DeviceIdType.MESH).start()

    loads = [pltpu.make_async_copy(hbm, ref, local_sem.at[i]) for i, (hbm, ref) in enumerate((
        (routes_hbm, routes_ref), (gates_hbm, gates_ref), (tok_hbm, tok_ref), (aup_hbm, aup_ref), (bdn_hbm, bdn_ref),
        (wup_hbm, wraw), (wdn_hbm, wdraw), (bup_hbm, bup_ref), (adn_hbm, adn_ref)))]
    for load in loads:
        load.start()
    load_up, load_down, load_bup, load_adn = loads[5:]

    barrier = pltpu.get_barrier_semaphore()

    def greet(device):
        pl.semaphore_signal(barrier, inc=1, device_id=device, device_id_type=pl.DeviceIdType.MESH)

    greet(at(z, y, 1 - core))

    @pl.loop(1, NY)
    def _(j):
        for cc in range(2):
            greet(at(z, (y + j) % NY, cc))

    @pl.loop(1, NZ)
    def _(j):
        for cc in range(2):
            greet(at((z + j) % NZ, y, cc))

    @pl.loop(1, NX)
    def _(j):
        greet({"tensor": (x + j) % NX})

    for load in loads[:3]:
        load.wait()
    tok2[0:quarter, :] = tok_ref[...]
    tok2[quarter:, :] = jnp.zeros_like(tok2[quarter:, :])

    before = (lax.broadcasted_iota(I32, (tokens, tokens), 0)
              < lax.broadcasted_iota(I32, (tokens, tokens), 1)).astype(F32).astype(BF16)
    slot_row = lax.broadcasted_iota(I32, (filled, tokens), 0)
    slot_of = (slot_row // NZ).astype(F32)
    none = jnp.zeros((padded - filled, tokens), F32)

    def expert_ids(p, i, cc):
        return (slot_row % NZ) * (2 if p else 2 * NY) + (i * (2 * NY if p else 2) + cc)

    def fill(table, p):
        for i in range(NY):
            for cc in range(2):
                hit = jnp.zeros((filled, tokens), F32)
                for k in range(4):
                    hit = jnp.where(routes_ref[k:k + 1, :] == expert_ids(p, i, cc), 1.0, hit)
                position = dot(hit.astype(BF16), before, NN)
                pick = jnp.where(position == slot_of, hit, 0.0)
                first = (2 * i + cc) * padded
                table[first:first + padded, :] = jnp.concatenate([pick, none], axis=0).astype(BF16)

    def weigh():
        for p, chosen, table in ((0, sel, gain), (1, selz, gainz)):
            for i in range(NY):
                for cc in range(2):
                    gate = jnp.zeros((filled, tokens), I32)
                    for k in range(4):
                        gate = jnp.where(routes_ref[k:k + 1, :] == expert_ids(p, i, cc), gates_ref[k:k + 1, :], gate)
                    first = (2 * i + cc) * padded
                    pick = chosen[first:first + padded, :]
                    high = (gate >> 8).astype(F32) * (1.0 / 256.0)
                    low = (gate & 255).astype(F32) * (1.0 / 65536.0)
                    table[first:first + padded, 0:tokens] = pick * jnp.concatenate([high, none], axis=0).astype(BF16)
                    table[first:first + padded, tokens:] = pick * jnp.concatenate([low, none], axis=0).astype(BF16)

    def order_merge():
        row = lax.broadcasted_iota(I32, (ygroup, spread_rows), 0)
        column = lax.broadcasted_iota(I32, (ygroup, spread_rows), 1)
        both_slot = row // NZ
        source = ((row % NZ) * 2 + both_slot // CAP) * padded + (both_slot % CAP) * NZ
        for a in range(NY):
            merge[a * ygroup:(a + 1) * ygroup, :] = (column == source + a).astype(F32).astype(BF16)

    def order_blocks():
        row = lax.broadcasted_iota(I32, (ygroup, rows), 0)
        column = lax.broadcasted_iota(I32, (ygroup, rows), 1)
        source = (row % NZ) * ygroup + (row // NZ) * NZ
        for a in range(NY):
            perm[a * ygroup:(a + 1) * ygroup, :] = (column == source + a).astype(F32).astype(BF16)

    def order_split():
        row = lax.broadcasted_iota(I32, (padded, rows), 0)
        column = lax.broadcasted_iota(I32, (padded, rows), 1)
        target = jnp.where(row < filled, (row % NZ) * ygroup + (row // NZ) * NZ, rows)
        for i in range(NY):
            for cc in range(2):
                first = (2 * i + cc) * padded
                split[first:first + padded, :] = (column == target + (cc * CAP * NZ + i)).astype(F32).astype(BF16)

    fill(sel, 0)
    fill(selz, 1)
    order_merge()
    ysend[0] = dot(sel[...], tok2[0:LANES, :], NT).astype(BF16)
    for load in loads[3:5]:
        load.wait()

    pl.semaphore_wait(barrier, 2 * NY + 2 * NZ + NX - 4)

    def exchange():
        mine = pl.ds(pl.multiple_of(x * part_rank, part_rank), part_rank)

        @pl.loop(1, NX)
        def _(j):
            send_one(aup_ref, afull.at[mine], UP_IN, {"tensor": (x + j) % NX})
            send_one(bdn_ref, bfull.at[x], DOWN_OUT, {"tensor": (x + j) % NX})

    def prepare():
        acc[...] = jnp.zeros_like(acc)
        hid[...] = jnp.zeros_like(hid)
        afull[pl.ds(pl.multiple_of(x * part_rank, part_rank), part_rank), :] = aup_ref[...]
        bfull[x] = bdn_ref[...]

    place = (y, z)

    def block(i):
        return pl.ds(pl.multiple_of(i * ygroup, 16), ygroup)

    def scatter(src, dst, axis, kind, k):
        @pl.loop(0, NY - 1)
        def _(n):
            i = (place[axis] + NY // 2 + (n + 1) // 2 * (1 - 2 * (n % 2))) % NY
            send(src.at[block(i)], dst.at[block(place[axis])], kind, k, at(z, i, core) if axis == 0 else at(i, y, core))

        dst[block(place[axis]), :] = src[block(place[axis]), :]

    def padded_block(i):
        return pl.ds(pl.multiple_of(i * padded, 16), padded)

    def scatter_both(src, dst, axis, kind, k):
        mine = 2 * place[axis] + core

        @pl.loop(0, 2 * NY - 1)
        def _(n):
            m = n // 2
            i = (place[axis] + NY // 2 + (m + 1) // 2 * (1 - 2 * (m % 2))) % NY
            last_one = n // (2 * NY - 2)
            i = i + (place[axis] - i) * last_one
            cc = n % 2 + (1 - core - n % 2) * last_one
            send(src.at[padded_block(2 * i + cc)], dst.at[padded_block(mine)], kind, k,
                 at(z, i, cc) if axis == 0 else at(i, y, cc))

        dst[padded_block(mine), :] = src[padded_block(mine), :]

    def choose(k, p, ready=False):
        feats = pl.ds(pl.multiple_of(k * LANES, LANES), LANES)
        if not ready:
            ysend[k] = dot((sel, selz)[p][...], tok2[feats, :], NT).astype(BF16)
        scatter_both(ysend.at[k], yrecv.at[k], p, OUT_1, k)

    def pass_on(k, p):
        arrived(yrecv.at[k, 0:spread_rows - padded], OUT_1, k)
        zsend[k] = dot(merge[...], yrecv[k], NN).astype(BF16)
        scatter(zsend.at[k], late.at[k] if p else gath.at[k, x], 1 - p, OUT_2, k)

    def span(h, scale=1):
        count = rows // scale
        return slice(0, count) if h is None else slice(h * count // 2, (h + 1) * count // 2)

    def slot(k, h):
        return k + chunks if h == 1 else k

    def ends(h):
        whole = span(h)
        middle = (whole.start + whole.stop) // 2
        return slice(whole.start, middle), slice(middle, whole.stop)

    def spread(k, p, h=None):
        if h != 1:
            arrived(late.at[k, 0:rows - ygroup], OUT_2, k)
            if p:
                gath[k, x] = dot(perm[...], late[k], NN).astype(BF16)
        mine = gath.at[k, x, span(h)]
        send(mine, mine, OUT_RIGHT, slot(k, h), {"tensor": right})
        send(mine, mine, OUT_LEFT, slot(k, h), {"tensor": left})

    def forward(k, h=None):
        top, bottom = ends(h)
        arrived(gath.at[k, left, span(h)], OUT_RIGHT, slot(k, h))
        send(gath.at[k, left, top], gath.at[k, left, top], OUT_RIGHT2, slot(k, h), {"tensor": right})
        arrived(gath.at[k, right, span(h)], OUT_LEFT, slot(k, h))
        send(gath.at[k, right, bottom], gath.at[k, right, bottom], OUT_LEFT2, slot(k, h), {"tensor": left})

    def multiply(k, h=None):
        top, bottom = ends(h)
        arrived(gath.at[k, across, top], OUT_RIGHT2, slot(k, h))
        arrived(gath.at[k, across, bottom], OUT_LEFT2, slot(k, h))
        lhs = jnp.concatenate([gath[k, q, span(h), :] for q in range(NX)], axis=1)
        acc[span(h), :] += dot(lhs, w1[k], NT)

    def arrange(raw, weights):
        for k in range(chunks):
            width = min(LANES, quarter - k * LANES)
            for q in range(NX):
                first = q * quarter + k * LANES
                weights[k, 0:hidden, q * LANES:q * LANES + width] = raw[0, :, first:first + width]

    def arrange_up():
        load_up.wait()
        w1[...] = jnp.zeros_like(w1)
        arrange(wraw, w1)

    def arrange_down():
        load_down.wait()
        w2[...] = jnp.zeros_like(w2)
        arrange(wdraw, w2)

    def arrange_adapters():
        pltpu.make_async_copy(afull.at[0:(NX - 1) * part_rank], afull.at[0:(NX - 1) * part_rank],
                              recv_once.at[UP_IN]).wait()
        pltpu.make_async_copy(bfull.at[0:NX - 1], bfull.at[0:NX - 1], recv_once.at[DOWN_OUT]).wait()
        for k in range(chunks):
            width = min(LANES, quarter - k * LANES)
            for q in range(NX):
                first = q * quarter + k * LANES
                w1[k, code_at:, q * LANES:q * LANES + width] = afull[:, first:first + width]
                w2[k, code_at:, q * LANES:q * LANES + width] = bfull[q, :, k * LANES:k * LANES + width]

    pairs = chunks // 2

    def step(tick, stage, delay, parity, *more):
        pair = tick - delay

        @pl.when((pair >= 0) & (pair < pairs))
        def _():
            stage(2 * pair + parity, *more)

    choose(0, 0, True)
    choose(1, 1)
    exchange()
    if pairs > 1:
        choose(2, 0)
        choose(3, 1)
    order_blocks()
    prepare()
    arrange_up()

    @pl.loop(0, pairs)
    def _(t):
        step(t, pass_on, 0, 0, 0)
        step(t, pass_on, 0, 1, 1)
        step(t, choose, -2, 0, 0)
        step(t, choose, -2, 1, 1)

        @pl.when(t == 0)
        def _():
            weigh()
            order_split()

        step(t, forward, 2, 0)
        step(t, spread, 1, 0, 0)
        step(t, spread, 1, 1, 1)

        @pl.when(t == min(1, pairs - 1))
        def _():
            arrange_down()
            arrange_adapters()

        step(t, forward, 2, 1)
        step(t, multiply, 3, 1)
        step(t, multiply, 2, 0)

    load_bup.wait()
    load_adn.wait()

    def activate(h):
        codes = acc[span(h), code_at:].astype(BF16)
        upward = acc[span(h), 0:hidden] + 0.5 * dot(codes, bup_ref[...], NN)
        units = (upward * jax.nn.sigmoid(1.702 * upward)).astype(BF16)
        hid[span(h), 0:hidden] = units
        hid[span(h), code_at:] = (0.5 * dot(units, adn_ref[...], NT)).astype(BF16)

    def partial(k, h=None):
        top, bottom = ends(h)
        product = dot(hid[span(h), :], w2[k], NN).astype(BF16)
        for q in range(NX):
            part[k, q, span(h), :] = product[:, q * LANES:(q + 1) * LANES]
        send(part.at[k, across, top], half_l.at[k, span(h, 2)], SUM_RIGHT, slot(k, h), {"tensor": right})
        send(part.at[k, across, bottom], half_r.at[k, span(h, 2)], SUM_LEFT, slot(k, h), {"tensor": left})

    def add_half(k, h=None):
        top, bottom = ends(h)
        half_of = span(h, 2)
        arrived(half_l.at[k, half_of], SUM_RIGHT, slot(k, h))
        part[k, right, top, :] = (part[k, right, top, :].astype(F32) + half_l[k, half_of, :].astype(F32)).astype(BF16)
        send(part.at[k, right, span(h)], full_l.at[k, span(h)], SUM_RIGHT2, slot(k, h), {"tensor": right})
        arrived(half_r.at[k, half_of], SUM_LEFT, slot(k, h))
        part[k, left, bottom, :] = (part[k, left, bottom, :].astype(F32)
                                    + half_r[k, half_of, :].astype(F32)).astype(BF16)
        send(part.at[k, left, span(h)], full_r.at[k, span(h)], SUM_LEFT2, slot(k, h), {"tensor": left})

    def add_full(k, p, h=None):
        where = span(h)
        arrived(full_l.at[k, where], SUM_RIGHT2, slot(k, h))
        arrived(full_r.at[k, where], SUM_LEFT2, slot(k, h))
        total[where, :] = (part[k, x, where, :].astype(F32) + full_l[k, where, :].astype(F32)
                           + full_r[k, where, :].astype(F32)).astype(BF16)
        if h != 0:
            esend[k] = dot(perm[...], total[...], NN).astype(BF16) if p else total[...]
            scatter(esend.at[k], zback.at[k], 1 - p, BACK_1, k)

    def pass_back(k, p):
        arrived(zback.at[k, 0:rows - ygroup], BACK_1, k)
        yback[k] = dot(split[...], zback[k], NN).astype(BF16)
        scatter_both(yback.at[k], rback.at[k], p, BACK_2, k)

    def mix(k, p):
        arrived(rback.at[k, 0:spread_rows - padded], BACK_2, k)
        both_parts = dot(rback[k], (gain, gainz)[p][...], TN)
        own[k] = both_parts[:, 0:tokens] + both_parts[:, tokens:]

    end = chunks - 2
    more = pairs > 1
    if more:
        forward(end - 2)
    spread(end, 0, 0)
    spread(end + 1, 1, 0)
    if more:
        forward(end - 1)
    spread(end, 0, 1)
    spread(end + 1, 1, 1)
    if pairs > 2:
        multiply(end - 3)
    if more:
        multiply(end - 2)
    forward(end, 0)
    forward(end + 1, 0)
    if more:
        multiply(end - 1)
    forward(end, 1)
    forward(end + 1, 1)
    for h in range(2):
        multiply(end, h)
        multiply(end + 1, h)
        activate(h)
        partial(0, h)
        partial(1, h)
    for h in range(2):
        add_half(0, h)
        add_half(1, h)
        if more:
            partial(2 + h)
    if more:
        add_half(2)
        if pairs > 2:
            partial(4)
    add_full(0, 0, 0)
    add_full(0, 0, 1)
    if more:
        add_half(3)
        if pairs > 2:
            partial(5)
    add_full(1, 1, 0)
    add_full(1, 1, 1)

    def tick(t):
        for p in range(2):
            step(t, add_half, 0, p)
            step(t, partial, -1, p)
            step(t, add_full, 1, p, p)
        step(t, pass_back, 2, 0, 0)
        step(t, pass_back, 2, 1, 1)
        step(t, mix, 3, 0, 0)
        step(t, mix, 3, 1, 1)

    @pl.loop(2, max(2, pairs + 2))
    def _(t):
        tick(t)

    @pl.loop(0, chunks)
    def _(k):
        sent(ysend.at[k, 0:spread_rows - padded], OUT_1, k)
        sent(zsend.at[k, 0:rows - ygroup], OUT_2, k)
        sent(esend.at[k, 0:rows - ygroup], BACK_1, k)

    for k in range(chunks):
        for h in (0, 1) if k >= end else (None,):
            top, bottom = ends(h)
            sent(gath.at[k, 0, span(h)], OUT_RIGHT, slot(k, h))
            sent(gath.at[k, 0, span(h)], OUT_LEFT, slot(k, h))
            sent(gath.at[k, 0, top], OUT_RIGHT2, slot(k, h))
            sent(gath.at[k, 0, bottom], OUT_LEFT2, slot(k, h))
        for h in (0, 1) if k < 2 else (None,):
            sent(half_l.at[k, span(h, 2)], SUM_RIGHT, slot(k, h))
            sent(half_r.at[k, span(h, 2)], SUM_LEFT, slot(k, h))
            sent(full_l.at[k, span(h)], SUM_RIGHT2, slot(k, h))
            sent(full_r.at[k, span(h)], SUM_LEFT2, slot(k, h))

    pltpu.make_async_copy(afull.at[0:(NX - 1) * part_rank], afull.at[0:(NX - 1) * part_rank],
                          send_once.at[UP_IN]).wait()
    pltpu.make_async_copy(bfull.at[0:NX - 1], bfull.at[0:NX - 1], send_once.at[DOWN_OUT]).wait()

    @pl.loop(max(2, pairs + 2), pairs + 3)
    def _(t):
        tick(t)

    for k in range(chunks):
        width = min(LANES, quarter - k * LANES)
        out_ref[k * LANES:k * LANES + width, :] = own[k, 0:width, :].astype(BF16)

    @pl.loop(0, chunks)
    def _(k):
        sent(yback.at[k, 0:spread_rows - padded], BACK_2, k)


def local(tokens, routes, gates, wup, wdn, aup, bup, adn, bdn):
    count, quarter = tokens.shape
    hidden, rank = wup.shape[2], bup.shape[1]
    part_rank = aup.shape[2]
    chunks = -(-quarter // LANES)
    rows = SLOTS * NY * NZ
    padded_rows = 2 * NY * (-(-CAP * NZ // 16) * 16)
    inner = -(-hidden // LANES) * LANES + rank
    grid = (chunks, rows, LANES)
    vmem, hbm = pl.BlockSpec(memory_space=pltpu.VMEM), pl.BlockSpec(memory_space=pl.ANY)
    out = pl.pallas_call(
        functools.partial(kernel, chunks),
        out_shape=jax.ShapeDtypeStruct((quarter, count), BF16),
        in_specs=[hbm] * 9,
        out_specs=vmem,
        scratch_shapes=[
            pltpu.VMEM((4, count), I32),
            pltpu.VMEM((4, count), I32),
            pltpu.VMEM((quarter, count), BF16),
            pltpu.VMEM((part_rank, NX * quarter), BF16),
            pltpu.VMEM((rank, hidden), BF16),
            pltpu.VMEM((rank, hidden), BF16),
            pltpu.VMEM((rank, quarter), BF16),
            pltpu.VMEM((chunks * LANES, count), BF16),
            pltpu.VMEM((padded_rows, count), BF16),
            pltpu.VMEM((padded_rows, count), BF16),
            pltpu.VMEM((padded_rows, 2 * count), BF16),
            pltpu.VMEM((padded_rows, 2 * count), BF16),
            pltpu.VMEM((rows, rows), BF16),
            pltpu.VMEM((rows, padded_rows), BF16),
            pltpu.VMEM((padded_rows, rows), BF16),
            pltpu.VMEM((1, hidden, NX * quarter), BF16),
            pltpu.VMEM((1, hidden, NX * quarter), BF16),
            pltpu.VMEM((rank, NX * quarter), BF16),
            pltpu.VMEM((NX, rank, quarter), BF16),
            pltpu.VMEM((chunks, inner, NX * LANES), BF16),
            pltpu.VMEM((chunks, inner, NX * LANES), BF16),
            pltpu.VMEM((chunks, padded_rows, LANES), BF16),
            pltpu.VMEM((chunks, padded_rows, LANES), BF16),
            pltpu.VMEM(grid, BF16),
            pltpu.VMEM(grid, BF16),
            pltpu.VMEM((chunks, NX, rows, LANES), BF16),
            pltpu.VMEM((rows, inner), F32),
            pltpu.VMEM((rows, inner), BF16),
            pltpu.VMEM((chunks, NX, rows, LANES), BF16),
            pltpu.VMEM((chunks, rows // 2, LANES), BF16),
            pltpu.VMEM((chunks, rows // 2, LANES), BF16),
            pltpu.VMEM(grid, BF16),
            pltpu.VMEM(grid, BF16),
            pltpu.VMEM((rows, LANES), BF16),
            pltpu.VMEM(grid, BF16),
            pltpu.VMEM(grid, BF16),
            pltpu.VMEM((chunks, padded_rows, LANES), BF16),
            pltpu.VMEM((chunks, padded_rows, LANES), BF16),
            pltpu.VMEM((chunks, LANES, count), F32),
            pltpu.SemaphoreType.DMA((KINDS, 2 * chunks)),
            pltpu.SemaphoreType.DMA((KINDS, 2 * chunks)),
            pltpu.SemaphoreType.DMA((2,)),
            pltpu.SemaphoreType.DMA((2,)),
            pltpu.SemaphoreType.DMA((9,)),
        ],
        compiler_params=pltpu.CompilerParams(
            collective_id=0, has_side_effects=True, vmem_limit_bytes=60 * 1024 * 1024),
        cost_estimate=pl.CostEstimate(flops=8 * 10**9, bytes_accessed=6 * 10**6, transcendentals=0),
    )(routes.T, gates.T, tokens.T, jnp.swapaxes(wup, 1, 2), wdn, aup[0].T, bup[0], adn[0].T, bdn[0])
    return out.T


def solution(mesh):
    return jax.shard_map(
        local,
        mesh=mesh,
        in_specs=(
            P("expert", "tensor"),
            P("expert", None),
            P("expert", None),
            P("expert", None, "tensor"),
            P("expert", "tensor", None),
            P("expert", None, "tensor"),
            P("expert", None, "tensor"),
            P("expert", "tensor", None),
            P("expert", None, "tensor"),
        ),
        out_specs=P("expert", "tensor"),
        check_vma=False,
    )
```

```python
import functools

import jax
import jax.numpy as jnp
from jax import lax
from jax.experimental import pallas as pl
from jax.experimental.pallas import tpu as pltpu
from jax.sharding import PartitionSpec as P

NZ, NY, NX = 8, 8, 4
CAP = 5
SLOTS = 2 * CAP
LANES = 128
BF16, F32, I32 = jnp.bfloat16, jnp.float32, jnp.int32

NN = (((1,), (0,)), ((), ()))
NT = (((1,), (1,)), ((), ()))
TN = (((0,), (0,)), ((), ()))

(OUT_1, OUT_2, OUT_RIGHT, OUT_LEFT, OUT_RIGHT2, OUT_LEFT2, SUM_RIGHT, SUM_LEFT, SUM_RIGHT2, SUM_LEFT2,
 BACK_1, BACK_2, KINDS) = range(13)
UP_IN, DOWN_OUT = range(2)


def dot(a, b, dims):
    return lax.dot_general(a, b, dims, preferred_element_type=F32)


def kernel(chunks, routes_hbm, gates_hbm, tok_hbm, wup_hbm, wdn_hbm, aup_hbm, bup_hbm, adn_hbm, bdn_hbm, out_ref,
           routes_ref, gates_ref, tok_ref, aup_ref, bup_ref, adn_ref, bdn_ref, tok2, sel, selz, gain, gainz, perm, merge, split, wraw, wdraw, afull, bfull, w1, w2,
           ysend, yrecv, zsend, late, gath, acc, hid, part, half_l, half_r, full_l, full_r,
           total, esend, zback, yback, rback, own,
           send_sem, recv_sem, send_once, recv_once, local_sem):
    expert, x = lax.axis_index("expert"), lax.axis_index("tensor")
    z, y, core = expert // (2 * NY), (expert // 2) % NY, expert % 2
    right, left, across = (x + 1) % NX, (x + NX - 1) % NX, (x + 2) % NX
    quarter, tokens = tok_ref.shape
    hidden = bup_ref.shape[1]
    rank = bup_ref.shape[0]
    part_rank = aup_ref.shape[0]
    code_at = w1.shape[1] - rank
    ygroup = SLOTS * NZ
    rows = ygroup * NY
    half = rows // 2
    filled = CAP * NZ
    padded = -(-filled // 16) * 16
    spread_rows = 2 * NY * padded
    last = quarter - (chunks - 1) * LANES

    def at(zz, yy, cc):
        return {"expert": (zz * NY + yy) * 2 + cc}

    def send(src, dst, kind, k, device):
        pltpu.make_async_remote_copy(
            src_ref=src, dst_ref=dst, send_sem=send_sem.at[kind, k], recv_sem=recv_sem.at[kind, k],
            device_id=device, device_id_type=pl.DeviceIdType.MESH).start()

    def arrived(ref, kind, k):
        pltpu.make_async_copy(ref, ref, recv_sem.at[kind, k]).wait()

    def sent(ref, kind, k):
        pltpu.make_async_copy(ref, ref, send_sem.at[kind, k]).wait()

    def send_one(src, dst, which, device):
        pltpu.make_async_remote_copy(
            src_ref=src, dst_ref=dst, send_sem=send_once.at[which], recv_sem=recv_once.at[which],
            device_id=device, device_id_type=pl.DeviceIdType.MESH).start()

    loads = [pltpu.make_async_copy(hbm, ref, local_sem.at[i]) for i, (hbm, ref) in enumerate((
        (routes_hbm, routes_ref), (gates_hbm, gates_ref), (tok_hbm, tok_ref), (aup_hbm, aup_ref), (bdn_hbm, bdn_ref),
        (wup_hbm, wraw), (wdn_hbm, wdraw), (bup_hbm, bup_ref), (adn_hbm, adn_ref)))]
    for load in loads:
        load.start()
    load_up, load_down, load_bup, load_adn = loads[5:]

    barrier = pltpu.get_barrier_semaphore()

    def greet(device):
        pl.semaphore_signal(barrier, inc=1, device_id=device, device_id_type=pl.DeviceIdType.MESH)

    greet(at(z, y, 1 - core))

    @pl.loop(1, NY)
    def _(j):
        for cc in range(2):
            greet(at(z, (y + j) % NY, cc))

    @pl.loop(1, NZ)
    def _(j):
        for cc in range(2):
            greet(at((z + j) % NZ, y, cc))

    @pl.loop(1, NX)
    def _(j):
        greet({"tensor": (x + j) % NX})

    for load in loads[:3]:
        load.wait()
    tok2[0:quarter, :] = tok_ref[...]
    tok2[quarter:, :] = jnp.zeros_like(tok2[quarter:, :])

    before = (lax.broadcasted_iota(I32, (tokens, tokens), 0)
              < lax.broadcasted_iota(I32, (tokens, tokens), 1)).astype(F32).astype(BF16)
    slot_row = lax.broadcasted_iota(I32, (filled, tokens), 0)
    slot_of = (slot_row // NZ).astype(F32)
    none = jnp.zeros((padded - filled, tokens), F32)

    def expert_ids(p, i, cc):
        return (slot_row % NZ) * (2 if p else 2 * NY) + (i * (2 * NY if p else 2) + cc)

    def fill(table, p):
        for i in range(NY):
            for cc in range(2):
                hit = jnp.zeros((filled, tokens), F32)
                for k in range(4):
                    hit = jnp.where(routes_ref[k:k + 1, :] == expert_ids(p, i, cc), 1.0, hit)
                position = dot(hit.astype(BF16), before, NN)
                pick = jnp.where(position == slot_of, hit, 0.0)
                first = (2 * i + cc) * padded
                table[first:first + padded, :] = jnp.concatenate([pick, none], axis=0).astype(BF16)

    def weigh():
        for p, chosen, table in ((0, sel, gain), (1, selz, gainz)):
            for i in range(NY):
                for cc in range(2):
                    gate = jnp.zeros((filled, tokens), I32)
                    for k in range(4):
                        gate = jnp.where(routes_ref[k:k + 1, :] == expert_ids(p, i, cc), gates_ref[k:k + 1, :], gate)
                    first = (2 * i + cc) * padded
                    pick = chosen[first:first + padded, :]
                    high = (gate >> 8).astype(F32) * (1.0 / 256.0)
                    low = (gate & 255).astype(F32) * (1.0 / 65536.0)
                    table[first:first + padded, 0:tokens] = pick * jnp.concatenate([high, none], axis=0).astype(BF16)
                    table[first:first + padded, tokens:] = pick * jnp.concatenate([low, none], axis=0).astype(BF16)

    def order_merge():
        row = lax.broadcasted_iota(I32, (ygroup, spread_rows), 0)
        column = lax.broadcasted_iota(I32, (ygroup, spread_rows), 1)
        both_slot = row // NZ
        source = ((row % NZ) * 2 + both_slot // CAP) * padded + (both_slot % CAP) * NZ
        for a in range(NY):
            merge[a * ygroup:(a + 1) * ygroup, :] = (column == source + a).astype(F32).astype(BF16)

    def order_blocks():
        row = lax.broadcasted_iota(I32, (ygroup, rows), 0)
        column = lax.broadcasted_iota(I32, (ygroup, rows), 1)
        source = (row % NZ) * ygroup + (row // NZ) * NZ
        for a in range(NY):
            perm[a * ygroup:(a + 1) * ygroup, :] = (column == source + a).astype(F32).astype(BF16)

    def order_split():
        row = lax.broadcasted_iota(I32, (padded, rows), 0)
        column = lax.broadcasted_iota(I32, (padded, rows), 1)
        target = jnp.where(row < filled, (row % NZ) * ygroup + (row // NZ) * NZ, rows)
        for i in range(NY):
            for cc in range(2):
                first = (2 * i + cc) * padded
                split[first:first + padded, :] = (column == target + (cc * CAP * NZ + i)).astype(F32).astype(BF16)

    fill(sel, 0)
    fill(selz, 1)
    order_merge()
    ysend[0] = dot(sel[...], tok2[0:LANES, :], NT).astype(BF16)
    for load in loads[3:5]:
        load.wait()

    pl.semaphore_wait(barrier, 2 * NY + 2 * NZ + NX - 4)

    def exchange():
        mine = pl.ds(pl.multiple_of(x * part_rank, part_rank), part_rank)

        @pl.loop(1, NX)
        def _(j):
            send_one(aup_ref, afull.at[mine], UP_IN, {"tensor": (x + j) % NX})
            send_one(bdn_ref, bfull.at[x], DOWN_OUT, {"tensor": (x + j) % NX})

    def prepare():
        acc[...] = jnp.zeros_like(acc)
        hid[...] = jnp.zeros_like(hid)
        afull[pl.ds(pl.multiple_of(x * part_rank, part_rank), part_rank), :] = aup_ref[...]
        bfull[x] = bdn_ref[...]

    place = (y, z)

    def block(i):
        return pl.ds(pl.multiple_of(i * ygroup, 16), ygroup)

    def scatter(src, dst, axis, kind, k):
        @pl.loop(0, NY - 1)
        def _(n):
            i = (place[axis] + NY // 2 + (n + 1) // 2 * (1 - 2 * (n % 2))) % NY
            send(src.at[block(i)], dst.at[block(place[axis])], kind, k, at(z, i, core) if axis == 0 else at(i, y, core))

        dst[block(place[axis]), :] = src[block(place[axis]), :]

    def padded_block(i):
        return pl.ds(pl.multiple_of(i * padded, 16), padded)

    def scatter_both(src, dst, axis, kind, k):
        mine = 2 * place[axis] + core

        @pl.loop(0, 2 * NY - 1)
        def _(n):
            m = n // 2
            i = (place[axis] + NY // 2 + (m + 1) // 2 * (1 - 2 * (m % 2))) % NY
            last_one = n // (2 * NY - 2)
            i = i + (place[axis] - i) * last_one
            cc = n % 2 + (1 - core - n % 2) * last_one
            send(src.at[padded_block(2 * i + cc)], dst.at[padded_block(mine)], kind, k,
                 at(z, i, cc) if axis == 0 else at(i, y, cc))

        dst[padded_block(mine), :] = src[padded_block(mine), :]

    def choose(k, p, ready=False):
        feats = pl.ds(pl.multiple_of(k * LANES, LANES), LANES)
        if not ready:
            ysend[k] = dot((sel, selz)[p][...], tok2[feats, :], NT).astype(BF16)
        scatter_both(ysend.at[k], yrecv.at[k], p, OUT_1, k)

    def pass_on(k, p):
        arrived(yrecv.at[k, 0:spread_rows - padded], OUT_1, k)
        zsend[k] = dot(merge[...], yrecv[k], NN).astype(BF16)
        scatter(zsend.at[k], late.at[k] if p else gath.at[k, x], 1 - p, OUT_2, k)

    def span(h, scale=1):
        count = rows // scale
        return slice(0, count) if h is None else slice(h * count // 2, (h + 1) * count // 2)

    def slot(k, h):
        return k + chunks if h == 1 else k

    def ends(h):
        whole = span(h)
        middle = (whole.start + whole.stop) // 2
        return slice(whole.start, middle), slice(middle, whole.stop)

    def spread(k, p, h=None):
        if h != 1:
            arrived(late.at[k, 0:rows - ygroup], OUT_2, k)
            if p:
                gath[k, x] = dot(perm[...], late[k], NN).astype(BF16)
        mine = gath.at[k, x, span(h)]
        send(mine, mine, OUT_RIGHT, slot(k, h), {"tensor": right})
        send(mine, mine, OUT_LEFT, slot(k, h), {"tensor": left})

    def forward(k, h=None):
        top, bottom = ends(h)
        arrived(gath.at[k, left, span(h)], OUT_RIGHT, slot(k, h))
        send(gath.at[k, left, top], gath.at[k, left, top], OUT_RIGHT2, slot(k, h), {"tensor": right})
        arrived(gath.at[k, right, span(h)], OUT_LEFT, slot(k, h))
        send(gath.at[k, right, bottom], gath.at[k, right, bottom], OUT_LEFT2, slot(k, h), {"tensor": left})

    def multiply(k, h=None):
        top, bottom = ends(h)
        arrived(gath.at[k, across, top], OUT_RIGHT2, slot(k, h))
        arrived(gath.at[k, across, bottom], OUT_LEFT2, slot(k, h))
        lhs = jnp.concatenate([gath[k, q, span(h), :] for q in range(NX)], axis=1)
        acc[span(h), :] += dot(lhs, w1[k], NT)

    def arrange(raw, weights):
        for k in range(chunks):
            width = min(LANES, quarter - k * LANES)
            for q in range(NX):
                first = q * quarter + k * LANES
                weights[k, 0:hidden, q * LANES:q * LANES + width] = raw[0, :, first:first + width]

    def arrange_up():
        load_up.wait()
        w1[...] = jnp.zeros_like(w1)
        arrange(wraw, w1)

    def arrange_down():
        load_down.wait()
        w2[...] = jnp.zeros_like(w2)
        arrange(wdraw, w2)

    def arrange_adapters():
        pltpu.make_async_copy(afull.at[0:(NX - 1) * part_rank], afull.at[0:(NX - 1) * part_rank],
                              recv_once.at[UP_IN]).wait()
        pltpu.make_async_copy(bfull.at[0:NX - 1], bfull.at[0:NX - 1], recv_once.at[DOWN_OUT]).wait()
        for k in range(chunks):
            width = min(LANES, quarter - k * LANES)
            for q in range(NX):
                first = q * quarter + k * LANES
                w1[k, code_at:, q * LANES:q * LANES + width] = afull[:, first:first + width]
                w2[k, code_at:, q * LANES:q * LANES + width] = bfull[q, :, k * LANES:k * LANES + width]

    pairs = chunks // 2

    def step(tick, stage, delay, parity, *more):
        pair = tick - delay

        @pl.when((pair >= 0) & (pair < pairs))
        def _():
            stage(2 * pair + parity, *more)

    choose(0, 0, True)
    choose(1, 1)
    exchange()
    if pairs > 1:
        choose(2, 0)
        choose(3, 1)
    order_blocks()
    prepare()
    arrange_up()

    @pl.loop(0, pairs)
    def _(t):
        step(t, pass_on, 0, 0, 0)
        step(t, pass_on, 0, 1, 1)
        step(t, choose, -2, 0, 0)
        step(t, choose, -2, 1, 1)

        step(t, forward, 2, 0)
        step(t, spread, 1, 0, 0)
        step(t, spread, 1, 1, 1)

        @pl.when(t == min(1, pairs - 1))
        def _():
            arrange_down()
            arrange_adapters()

        step(t, forward, 2, 1)
        step(t, multiply, 3, 1)
        step(t, multiply, 2, 0)

    load_bup.wait()
    load_adn.wait()

    def activate(h):
        codes = acc[span(h), code_at:].astype(BF16)
        upward = acc[span(h), 0:hidden] + 0.5 * dot(codes, bup_ref[...], NN)
        units = (upward * jax.nn.sigmoid(1.702 * upward)).astype(BF16)
        hid[span(h), 0:hidden] = units
        hid[span(h), code_at:] = (0.5 * dot(units, adn_ref[...], NT)).astype(BF16)

    def partial(k, h=None):
        top, bottom = ends(h)
        product = dot(hid[span(h), :], w2[k], NN).astype(BF16)
        for q in range(NX):
            part[k, q, span(h), :] = product[:, q * LANES:(q + 1) * LANES]
        send(part.at[k, across, top], half_l.at[k, span(h, 2)], SUM_RIGHT, slot(k, h), {"tensor": right})
        send(part.at[k, across, bottom], half_r.at[k, span(h, 2)], SUM_LEFT, slot(k, h), {"tensor": left})

    def add_half(k, h=None):
        top, bottom = ends(h)
        half_of = span(h, 2)
        arrived(half_l.at[k, half_of], SUM_RIGHT, slot(k, h))
        part[k, right, top, :] = (part[k, right, top, :].astype(F32) + half_l[k, half_of, :].astype(F32)).astype(BF16)
        send(part.at[k, right, span(h)], full_l.at[k, span(h)], SUM_RIGHT2, slot(k, h), {"tensor": right})
        arrived(half_r.at[k, half_of], SUM_LEFT, slot(k, h))
        part[k, left, bottom, :] = (part[k, left, bottom, :].astype(F32)
                                    + half_r[k, half_of, :].astype(F32)).astype(BF16)
        send(part.at[k, left, span(h)], full_r.at[k, span(h)], SUM_LEFT2, slot(k, h), {"tensor": left})

    def add_full(k, p, h=None):
        where = span(h)
        arrived(full_l.at[k, where], SUM_RIGHT2, slot(k, h))
        arrived(full_r.at[k, where], SUM_LEFT2, slot(k, h))
        total[where, :] = (part[k, x, where, :].astype(F32) + full_l[k, where, :].astype(F32)
                           + full_r[k, where, :].astype(F32)).astype(BF16)
        if h != 0:
            esend[k] = dot(perm[...], total[...], NN).astype(BF16) if p else total[...]
            scatter(esend.at[k], zback.at[k], 1 - p, BACK_1, k)

    def pass_back(k, p):
        arrived(zback.at[k, 0:rows - ygroup], BACK_1, k)
        yback[k] = dot(split[...], zback[k], NN).astype(BF16)
        scatter_both(yback.at[k], rback.at[k], p, BACK_2, k)

    def mix(k, p):
        arrived(rback.at[k, 0:spread_rows - padded], BACK_2, k)
        both_parts = dot(rback[k], (gain, gainz)[p][...], TN)
        own[k] = both_parts[:, 0:tokens] + both_parts[:, tokens:]

    end = chunks - 2
    more = pairs > 1
    if more:
        forward(end - 2)
    spread(end, 0, 0)
    spread(end + 1, 1, 0)
    if more:
        forward(end - 1)
    spread(end, 0, 1)
    spread(end + 1, 1, 1)
    if pairs > 2:
        multiply(end - 3)
    if more:
        multiply(end - 2)
    forward(end, 0)
    forward(end + 1, 0)
    if more:
        multiply(end - 1)
    forward(end, 1)
    forward(end + 1, 1)
    for h in range(2):
        multiply(end, h)
        multiply(end + 1, h)
        activate(h)
        partial(0, h)
        partial(1, h)
    for h in range(2):
        add_half(0, h)
        add_half(1, h)
        if more:
            partial(2 + h)
    if more:
        add_half(2)
        if pairs > 2:
            partial(4)
    order_split()
    add_full(0, 0, 0)
    add_full(0, 0, 1)
    if more:
        add_half(3)
        if pairs > 2:
            partial(5)
    weigh()
    add_full(1, 1, 0)
    add_full(1, 1, 1)

    def tick(t):
        for p in range(2):
            step(t, add_half, 0, p)
            step(t, partial, -1, p)
            step(t, add_full, 1, p, p)
        step(t, pass_back, 2, 0, 0)
        step(t, pass_back, 2, 1, 1)
        step(t, mix, 3, 0, 0)
        step(t, mix, 3, 1, 1)

    @pl.loop(2, max(2, pairs + 2))
    def _(t):
        tick(t)

    @pl.loop(0, chunks)
    def _(k):
        sent(ysend.at[k, 0:spread_rows - padded], OUT_1, k)
        sent(zsend.at[k, 0:rows - ygroup], OUT_2, k)
        sent(esend.at[k, 0:rows - ygroup], BACK_1, k)

    for k in range(chunks):
        for h in (0, 1) if k >= end else (None,):
            top, bottom = ends(h)
            sent(gath.at[k, 0, span(h)], OUT_RIGHT, slot(k, h))
            sent(gath.at[k, 0, span(h)], OUT_LEFT, slot(k, h))
            sent(gath.at[k, 0, top], OUT_RIGHT2, slot(k, h))
            sent(gath.at[k, 0, bottom], OUT_LEFT2, slot(k, h))
        for h in (0, 1) if k < 2 else (None,):
            sent(half_l.at[k, span(h, 2)], SUM_RIGHT, slot(k, h))
            sent(half_r.at[k, span(h, 2)], SUM_LEFT, slot(k, h))
            sent(full_l.at[k, span(h)], SUM_RIGHT2, slot(k, h))
            sent(full_r.at[k, span(h)], SUM_LEFT2, slot(k, h))

    pltpu.make_async_copy(afull.at[0:(NX - 1) * part_rank], afull.at[0:(NX - 1) * part_rank],
                          send_once.at[UP_IN]).wait()
    pltpu.make_async_copy(bfull.at[0:NX - 1], bfull.at[0:NX - 1], send_once.at[DOWN_OUT]).wait()

    @pl.loop(max(2, pairs + 2), pairs + 3)
    def _(t):
        tick(t)

    for k in range(chunks):
        width = min(LANES, quarter - k * LANES)
        out_ref[k * LANES:k * LANES + width, :] = own[k, 0:width, :].astype(BF16)

    @pl.loop(0, chunks)
    def _(k):
        sent(yback.at[k, 0:spread_rows - padded], BACK_2, k)


def local(tokens, routes, gates, wup, wdn, aup, bup, adn, bdn):
    count, quarter = tokens.shape
    hidden, rank = wup.shape[2], bup.shape[1]
    part_rank = aup.shape[2]
    chunks = -(-quarter // LANES)
    rows = SLOTS * NY * NZ
    padded_rows = 2 * NY * (-(-CAP * NZ // 16) * 16)
    inner = -(-hidden // LANES) * LANES + rank
    grid = (chunks, rows, LANES)
    vmem, hbm = pl.BlockSpec(memory_space=pltpu.VMEM), pl.BlockSpec(memory_space=pl.ANY)
    out = pl.pallas_call(
        functools.partial(kernel, chunks),
        out_shape=jax.ShapeDtypeStruct((quarter, count), BF16),
        in_specs=[hbm] * 9,
        out_specs=vmem,
        scratch_shapes=[
            pltpu.VMEM((4, count), I32),
            pltpu.VMEM((4, count), I32),
            pltpu.VMEM((quarter, count), BF16),
            pltpu.VMEM((part_rank, NX * quarter), BF16),
            pltpu.VMEM((rank, hidden), BF16),
            pltpu.VMEM((rank, hidden), BF16),
            pltpu.VMEM((rank, quarter), BF16),
            pltpu.VMEM((chunks * LANES, count), BF16),
            pltpu.VMEM((padded_rows, count), BF16),
            pltpu.VMEM((padded_rows, count), BF16),
            pltpu.VMEM((padded_rows, 2 * count), BF16),
            pltpu.VMEM((padded_rows, 2 * count), BF16),
            pltpu.VMEM((rows, rows), BF16),
            pltpu.VMEM((rows, padded_rows), BF16),
            pltpu.VMEM((padded_rows, rows), BF16),
            pltpu.VMEM((1, hidden, NX * quarter), BF16),
            pltpu.VMEM((1, hidden, NX * quarter), BF16),
            pltpu.VMEM((rank, NX * quarter), BF16),
            pltpu.VMEM((NX, rank, quarter), BF16),
            pltpu.VMEM((chunks, inner, NX * LANES), BF16),
            pltpu.VMEM((chunks, inner, NX * LANES), BF16),
            pltpu.VMEM((chunks, padded_rows, LANES), BF16),
            pltpu.VMEM((chunks, padded_rows, LANES), BF16),
            pltpu.VMEM(grid, BF16),
            pltpu.VMEM(grid, BF16),
            pltpu.VMEM((chunks, NX, rows, LANES), BF16),
            pltpu.VMEM((rows, inner), F32),
            pltpu.VMEM((rows, inner), BF16),
            pltpu.VMEM((chunks, NX, rows, LANES), BF16),
            pltpu.VMEM((chunks, rows // 2, LANES), BF16),
            pltpu.VMEM((chunks, rows // 2, LANES), BF16),
            pltpu.VMEM(grid, BF16),
            pltpu.VMEM(grid, BF16),
            pltpu.VMEM((rows, LANES), BF16),
            pltpu.VMEM(grid, BF16),
            pltpu.VMEM(grid, BF16),
            pltpu.VMEM((chunks, padded_rows, LANES), BF16),
            pltpu.VMEM((chunks, padded_rows, LANES), BF16),
            pltpu.VMEM((chunks, LANES, count), F32),
            pltpu.SemaphoreType.DMA((KINDS, 2 * chunks)),
            pltpu.SemaphoreType.DMA((KINDS, 2 * chunks)),
            pltpu.SemaphoreType.DMA((2,)),
            pltpu.SemaphoreType.DMA((2,)),
            pltpu.SemaphoreType.DMA((9,)),
        ],
        compiler_params=pltpu.CompilerParams(
            collective_id=0, has_side_effects=True, vmem_limit_bytes=60 * 1024 * 1024),
        cost_estimate=pl.CostEstimate(flops=8 * 10**9, bytes_accessed=6 * 10**6, transcendentals=0),
    )(routes.T, gates.T, tokens.T, jnp.swapaxes(wup, 1, 2), wdn, aup[0].T, bup[0], adn[0].T, bdn[0])
    return out.T


def solution(mesh):
    return jax.shard_map(
        local,
        mesh=mesh,
        in_specs=(
            P("expert", "tensor"),
            P("expert", None),
            P("expert", None),
            P("expert", None, "tensor"),
            P("expert", "tensor", None),
            P("expert", None, "tensor"),
            P("expert", None, "tensor"),
            P("expert", "tensor", None),
            P("expert", None, "tensor"),
        ),
        out_specs=P("expert", "tensor"),
        check_vma=False,
    )
```
